32 devices in a mesh: clip: 2 (over y), tm: 4 (over z), head: 2 (over x), sub: 2 (over core).
Axes of the slice: x: 2, y: 2, z: 4, core: 2. Of those that a mesh axis runs over, the one named last changes fastest.
Arguments:
- queries: bfloat16 [8, 256, 3072], P(('clip', 'tm'), None, ('head', 'sub')), parts along dimension 0, may hold values from -6 to 6, as said below
- keys: bfloat16 [8, 256, 3072], P(('clip', 'tm'), None, ('head', 'sub')), parts along dimension 0, may hold values from -6 to 6, as said below
- values: bfloat16 [8, 256, 3072], P(('clip', 'tm'), None, ('head', 'sub')), parts along dimension 0, may hold values from -6 to 6
- band_table: int32 [4, 4], replicated, may hold values from 0 to 3, as said below
- windows: int32 [7], replicated, may hold values from 1 to 128, as said below
- out_weight: bfloat16 [3072, 3072], P(('head', 'sub')), may hold values from -0.109375 to 0.109375
Outputs:
- mixed: bfloat16 [8, 256, 3072], P(('clip', 'tm'), ('head', 'sub')), parts along dimension 0
The draws below stay inside these ranges and needn't reach their ends.
There are 2 independent parts, one for each index of `clip`. The reference program is written for one: setup_inputs(seed, part) draws one part's arguments, and reference() takes and returns one part's arrays. A program takes and returns all parts, laid end to end along the dimension named above; an argument that names none is the same for every part. Nothing has to cross between parts.
Inputs may be any that keep to these rules, and one draw needn't show every extreme that they name: `queries`: entries of normal law within the range; some rows may be aligned with some key rows. `keys`: entries of normal law within the range; some rows may be aligned with some query rows. `band_table`: Symmetric; 0 exactly on the diagonal; off the diagonal, for frames at distance d it is floor(log2 d) + 1 or one more, never above 6; the pair of frames 0 and 3 takes the one more (up to 6). windows[0] = 128; for k >= 1, windows[k] lies between max(1, 64 // 2**k) and max(that + 1, 128 // 2**k + 1) - 1.
All inputs are finite; a program needn't handle non-finite values.
Results may differ from the reference program's by a relative error of at most 0.015.
Values may be sent and summed in bfloat16 or wider, within the bound.
No kernel may reach another device: no remote copies, remote signals or barrier semaphores. Data moves between devices by JAX's collectives and lax.ppermute only.
A program may use at most 64 MiB of HBM per device.

```python
import jax
import jax.numpy as jnp
from jax import lax

D = 3072
HEADS = 24
HEAD = 128
S = 256
NB = 7
FRAMES = 4


def paired_fields(key):
    shape = (FRAMES, S, HEADS * HEAD)
    query = jnp.clip(jax.random.normal(jax.random.fold_in(key, 11), shape, jnp.float32), -6.0, 6.0)
    keyset = jnp.clip(jax.random.normal(jax.random.fold_in(key, 12), shape, jnp.float32), -6.0, 6.0)
    return (query, keyset)


def draw_queries(key, part):
    return paired_fields(key)[0].astype(jnp.bfloat16)


def draw_keys(key, part):
    return paired_fields(key)[1].astype(jnp.bfloat16)


def draw_band_table(key, part):
    index = jnp.arange(FRAMES, dtype=jnp.int32)
    distance = jnp.abs(index[:, None] - index[None, :])
    base = jnp.zeros((FRAMES, FRAMES), jnp.int32)
    for power in range(16):
        base = base + (distance >= 1 << power).astype(jnp.int32)
    jitter = jax.random.randint(jax.random.fold_in(key, 21), (FRAMES, FRAMES), 0, 2).astype(jnp.int32)
    jitter = jnp.triu(jitter, 1)
    jitter = jitter.at[0, FRAMES - 1].set(1)
    jitter = jitter + jnp.transpose(jitter)
    band = jnp.minimum(base + jitter, NB - 1)
    return jnp.where(distance > 0, band, 0).astype(jnp.int32)


def draw_windows(key, part):
    levels = jnp.left_shift(jnp.ones((NB,), jnp.int32), jnp.arange(NB, dtype=jnp.int32))
    lowest = jnp.maximum(1, S // 4 // levels)
    highest = jnp.maximum(lowest + 1, S // 2 // levels + 1)
    spread = jax.random.randint(jax.random.fold_in(key, 31), (NB,), 0, 1 << 20).astype(jnp.int32)
    reach = lowest + spread % (highest - lowest)
    reach = reach.at[0].set(S // 2)
    return reach.astype(jnp.int32)


def block_levels(key, extent, pieces, smallest, high):
    level = 1.0
    for axis_at, blocks in pieces:
        steps = jax.random.uniform(jax.random.fold_in(jax.random.fold_in(key, 6), axis_at), (blocks,), jnp.float32, smallest / len(pieces), high / len(pieces))
        level = level * jnp.repeat(jnp.exp(steps), extent[axis_at] // blocks).reshape((-1,) + (1,) * (len(extent) - 1 - axis_at))
    return level


def scatter_about(stream_key, extent, scale, limit, cuts=(), kind=jnp.bfloat16):
    gain = block_levels(stream_key, extent, cuts, -0.22, 0.18) if cuts else 1.0
    drawn = jax.random.normal(stream_key, extent, jnp.float32) * scale * gain
    return jnp.minimum(jnp.maximum(drawn, -limit), limit).astype(kind)


def setup_inputs(seed: int = 0, part: int = 0) -> dict:
    key_list = jax.random.split(jax.random.key(seed), 7)
    own_keys = jax.random.split(jax.random.fold_in(key_list[6], part), 7)
    queries = draw_queries(jax.random.fold_in(jax.random.fold_in(key_list[6], part), 71), part)
    keys = draw_keys(jax.random.fold_in(jax.random.fold_in(key_list[6], part), 71), part)
    values = scatter_about(own_keys[2], (FRAMES, S, HEADS * HEAD), 1.0, 6.0, ((0, 4), (2, 4)))
    band_table = draw_band_table(jax.random.fold_in(key_list[6], 71), part)
    windows = draw_windows(jax.random.fold_in(key_list[6], 71), part)
    out_weight = scatter_about(key_list[5], (HEADS * HEAD, D), (HEADS * HEAD) ** -0.5, 0.109375, ((0, 4),))
    return {"queries": queries, "keys": keys, "values": values, "band_table": band_table, "windows": windows, "out_weight": out_weight}


def reference(queries, keys, values, band_table, windows, out_weight):
    heads = HEADS
    scale = HEAD ** -0.5
    key_all = keys.reshape(FRAMES * S, heads, HEAD).astype(jnp.float32)
    value_all = values.reshape(FRAMES * S, heads, HEAD).astype(jnp.float32)
    places = jnp.arange(S, dtype=jnp.int32)
    key_places = jnp.tile(places, FRAMES)
    key_frames = jnp.repeat(jnp.arange(FRAMES, dtype=jnp.int32), S)

    def one_frame(frame):
        query = lax.dynamic_index_in_dim(queries, frame, 0, keepdims=False)
        query = query.reshape(S, heads, HEAD).astype(jnp.float32)
        reach = windows[band_table[frame]]
        allowed = jnp.abs(places[:, None] - key_places[None, :]) <= reach[key_frames][None, :]
        scores = jnp.einsum("phd,qhd->hpq", query, key_all, precision=lax.Precision.HIGHEST) * scale
        masked = jnp.where(allowed[None], scores, jnp.float32(-1e30))
        top = jnp.max(masked, axis=-1, keepdims=True)
        weights = jnp.where(allowed[None], jnp.exp(scores - top), jnp.float32(0.0))
        total = jnp.sum(weights, axis=-1)
        rounded = lax.optimization_barrier(weights.astype(jnp.bfloat16)).astype(jnp.float32)
        numer = jnp.einsum("hpq,qhd->phd", rounded, value_all, precision=lax.Precision.HIGHEST)
        attended = numer / jnp.transpose(total)[:, :, None]
        return attended.reshape(S, heads * HEAD).astype(jnp.bfloat16)

    attended = lax.map(one_frame, jnp.arange(FRAMES, dtype=jnp.int32))
    mixed = jnp.dot(attended.reshape(FRAMES * S, heads * HEAD), out_weight, preferred_element_type=jnp.float32)
    return mixed.astype(jnp.bfloat16).reshape(FRAMES, S, D)
```

```python
import functools

import jax
import jax.numpy as jnp
from jax import lax
from jax.experimental import pallas as pl
from jax.experimental.pallas import tpu as pltpu
from jax.sharding import PartitionSpec as P

HEAD = 128
ANY = pl.BlockSpec(memory_space=pl.ANY)
SMEM = pl.BlockSpec(memory_space=pltpu.SMEM)


def gathered(queries, keys, values, band_table, windows, out_weight):
    frames, length, width = queries.shape
    heads = width // HEAD
    scale = HEAD ** (-0.5)
    here = lax.axis_index("tm") * frames
    query = queries[0].reshape(length, heads, HEAD)
    places = lax.iota(jnp.int32, length)
    gap = jnp.abs(places[:, None] - places[None, :])

    def absorb(carry, key_frame, value_frame, frame):
        peak, total, numer = carry
        reach = windows[band_table[here, frame]]
        allowed = (gap <= reach)[None]
        scores = (
            jnp.einsum(
                "phd,qhd->hpq",
                query,
                key_frame.reshape(length, heads, HEAD),
                preferred_element_type=jnp.float32,
            )
            * scale
        )
        masked = jnp.where(allowed, scores, jnp.float32(-1e30))
        top = jnp.maximum(peak, jnp.max(masked, axis=-1))
        weights = jnp.where(allowed, jnp.exp(scores - top[:, :, None]), jnp.float32(0.0))
        shrink = jnp.exp(peak - top)
        total = total * shrink + jnp.sum(weights, axis=-1)
        added = jnp.einsum(
            "hpq,qhd->phd",
            weights.astype(jnp.bfloat16),
            value_frame.reshape(length, heads, HEAD),
            preferred_element_type=jnp.float32,
        )
        numer = numer * jnp.transpose(shrink)[:, :, None] + added
        return (top, total, numer)

    carry = (
        jnp.full((heads, length), -1e30, jnp.float32),
        jnp.zeros((heads, length), jnp.float32),
        jnp.zeros((length, heads, HEAD), jnp.float32),
    )
    key_part = lax.all_gather(keys, "tm", axis=0, tiled=True)
    value_part = lax.all_gather(values, "tm", axis=0, tiled=True)

    def advance(inner, item):
        return (absorb(inner, *item), None)

    state, _ = lax.scan(
        advance, carry, (key_part, value_part, lax.iota(jnp.int32, key_part.shape[0]))
    )
    _, total, numer = state
    attended = (
        (numer / jnp.transpose(total)[:, :, None]).astype(jnp.bfloat16).reshape(length, width)
    )
    mixed = lax.psum_scatter(
        jnp.dot(attended, out_weight, preferred_element_type=jnp.float32).astype(jnp.bfloat16),
        ("head", "sub"),
        scatter_dimension=0,
        tiled=True,
    )
    return mixed[None]


def run_copies(copies, sem):
    started = [pltpu.make_async_copy(s, d, sem.at[i]) for i, (s, d) in enumerate(copies)]
    for copy in started:
        copy.start()
    for copy in started:
        copy.wait()


def pack_kernel(n, cores, tokens, q_ref, k_ref, v_ref, *rest):
    kv_out, q_out, sem = rest[:n], rest[n : 2 * n], rest[2 * n]
    z = lax.axis_index("tm")
    wide = kv_out[0].shape[2]
    half = kv_out[0].shape[1]
    copies = []
    for r in range(n):
        t = z ^ r
        cols = pl.ds(pl.multiple_of((t // cores) * wide, wide), wide)
        b = t % cores
        rows = pl.ds(pl.multiple_of(b * half, half), half)
        copies.append((k_ref.at[0, rows, cols], kv_out[r].at[0]))
        copies.append((v_ref.at[0, rows, cols], kv_out[r].at[1]))
        for x in range(half // tokens):
            place = pl.ds(pl.multiple_of((x * cores + b) * tokens, tokens), tokens)
            copies.append((q_ref.at[0, place, cols], q_out[r].at[pl.ds(x * tokens, tokens)]))
    run_copies(copies, sem)


def attend_kernel(n, cores, tokens, band_ref, reach_ref, *rest):
    own, other, query = rest[:n], rest[n : 2 * n], rest[2 * n : 3 * n]
    outs = rest[3 * n : 4 * n]
    k_all, v_all, q_all, o_all, gap_ref, sem = rest[4 * n :]
    z, c = lax.axis_index("tm"), lax.axis_index("sub")
    half = own[0].shape[1]
    heads = own[0].shape[2] // HEAD
    length = half * cores
    t = (z % (n // cores)) * cores + c
    mine = pl.ds(pl.multiple_of(c * half, half), half)
    theirs = pl.ds(pl.multiple_of((1 - c) * half, half), half)
    copies = []
    for r in range(n):
        f = t ^ r
        copies.append((own[r].at[0], k_all.at[f, mine]))
        copies.append((own[r].at[1], v_all.at[f, mine]))
        copies.append((other[r].at[0], k_all.at[f ^ 1, theirs]))
        copies.append((other[r].at[1], v_all.at[f ^ 1, theirs]))
        copies.append((query[r], q_all.at[f]))
    run_copies(copies, sem)

    row = lax.broadcasted_iota(jnp.int32, (half, length), 0)
    place = (row // tokens * cores + c) * tokens + row % tokens
    gap_ref[...] = jnp.abs(place - lax.broadcasted_iota(jnp.int32, (half, length), 1))
    scale = jnp.float32(HEAD ** (-0.5))

    def frame(i, _):
        for h in range(heads):
            cols = slice(h * HEAD, (h + 1) * HEAD)
            q = q_all[i, :, cols]
            scores = []
            for j in range(n):
                reach = reach_ref[band_ref[i, j]]
                s = lax.dot_general(
                    q, k_all[j, :, cols], (((1,), (1,)), ((), ())),
                    preferred_element_type=jnp.float32,
                )
                scores.append(jnp.where(gap_ref[...] <= reach, s * scale, jnp.float32(-1e30)))
            top = jnp.max(functools.reduce(jnp.maximum, scores), axis=1, keepdims=True)
            weights = [jnp.exp(s - top) for s in scores]
            total = jnp.sum(functools.reduce(jnp.add, weights), axis=1, keepdims=True)
            numer = 0.0
            for j in range(n):
                numer += jnp.dot(
                    weights[j].astype(jnp.bfloat16), v_all[j, :, cols],
                    preferred_element_type=jnp.float32,
                )
            o_all[i, :, cols] = (numer / total).astype(jnp.bfloat16)
        return 0

    lax.fori_loop(0, n, frame, 0)
    run_copies([(o_all.at[z ^ k], outs[k]) for k in range(n)], sem)


def project_kernel(n, cores, tokens, own_w, other_w, *rest):
    parts = rest[:n]
    keep_ref, send_ref, a_all, sem = rest[n:]
    z, c, x = lax.axis_index("tm"), lax.axis_index("sub"), lax.axis_index("head")
    run_copies([(parts[k], a_all.at[z ^ k]) for k in range(n)], sem)
    per = n // cores
    wide = a_all.shape[2]

    def rows(x_of):
        at = pl.ds(pl.multiple_of(x_of * tokens, tokens), tokens)
        total = 0.0
        for w_ref, core in ((own_w, c), (other_w, 1 - c)):
            for g in range(per):
                total += jnp.dot(
                    a_all[core * per + g, at, :], w_ref[g * wide : (g + 1) * wide, :],
                    preferred_element_type=jnp.float32,
                )
        return total

    send_ref[...] = rows(1 - x).astype(send_ref.dtype)
    keep_ref[...] = rows(x)


def add_kernel(keep_ref, got_ref, out_ref):
    out_ref[0] = (keep_ref[...] + got_ref[...].astype(jnp.float32)).astype(out_ref.dtype)


def swapped(x, axis):
    return lax.ppermute(x, axis, [(0, 1), (1, 0)])


def spread(n, cores, queries, keys, values, band_table, windows, out_weight):
    _, length, width = queries.shape
    depth, model = out_weight.shape
    wide = width * cores // n
    half = length // cores
    tokens = half // 2
    bf16 = queries.dtype
    hbm = pl.ANY

    other_weight = swapped(out_weight, "sub")
    packed = pl.pallas_call(
        functools.partial(pack_kernel, n, cores, tokens),
        out_shape=[jax.ShapeDtypeStruct((2, half, wide), bf16)] * n
        + [jax.ShapeDtypeStruct((half, wide), bf16)] * n,
        in_specs=[ANY] * 3,
        out_specs=[ANY] * (2 * n),
        scratch_shapes=[pltpu.SemaphoreType.DMA((4 * n,))],
        name="pack",
    )(queries, keys, values)

    per = n // cores
    own, query = [], []
    for got, blocks in ((own, packed[:n]), (query, packed[n:])):
        for r in range(n):
            pairs = []
            for z in range(n):
                for c in range(cores):
                    t = z ^ r
                    pairs.append((z * cores + c, (c * per + t // cores) * cores + t % cores))
            got.append(lax.ppermute(blocks[r], ("tm", "sub"), pairs))
    other = [swapped(block, "sub") for block in own]

    outs = pl.pallas_call(
        functools.partial(attend_kernel, n, cores, tokens),
        out_shape=[jax.ShapeDtypeStruct((half, wide), bf16)] * n,
        in_specs=[SMEM, SMEM] + [ANY] * (3 * n),
        out_specs=[ANY] * n,
        scratch_shapes=[
            pltpu.VMEM((n, length, wide), bf16),
            pltpu.VMEM((n, length, wide), bf16),
            pltpu.VMEM((n, half, wide), bf16),
            pltpu.VMEM((n, half, wide), bf16),
            pltpu.VMEM((half, length), jnp.int32),
            pltpu.SemaphoreType.DMA((5 * n,)),
        ],
        compiler_params=pltpu.CompilerParams(vmem_limit_bytes=32 * 2**20),
        name="attend",
    )(band_table, windows, *own, *other, *query)

    parts = [outs[0]] + [
        lax.ppermute(outs[k], "tm", [(z, z ^ k) for z in range(n)]) for k in range(1, n)
    ]
    vmem = pl.BlockSpec(memory_space=pltpu.VMEM)
    keep, send = pl.pallas_call(
        functools.partial(project_kernel, n, cores, tokens),
        out_shape=[
            jax.ShapeDtypeStruct((tokens, model), jnp.float32),
            jax.ShapeDtypeStruct((tokens, model), bf16),
        ],
        in_specs=[vmem] * 2 + [ANY] * n,
        out_specs=[vmem] * 2,
        scratch_shapes=[
            pltpu.VMEM((n, half, wide), bf16),
            pltpu.SemaphoreType.DMA((n,)),
        ],
        compiler_params=pltpu.CompilerParams(vmem_limit_bytes=32 * 2**20),
        name="project",
    )(out_weight, other_weight, *parts)
    got = swapped(send, "head")
    return pl.pallas_call(
        add_kernel,
        out_shape=jax.ShapeDtypeStruct((1, tokens, model), bf16),
        in_specs=[vmem] * 2,
        out_specs=vmem,
        name="add",
    )(keep, got)


def solution(mesh):
    n, cores, xs = mesh.shape["tm"], mesh.shape["sub"], mesh.shape["head"]

    def local(queries, keys, values, band_table, windows, out_weight):
        frames, length, width = queries.shape
        fits = (
            frames == 1
            and n & (n - 1) == 0
            and cores == 2
            and xs == 2
            and n % cores == 0
            and width * cores % (n * HEAD) == 0
            and length % (xs * cores * 16) == 0
        )
        step = functools.partial(spread, n, cores) if fits else gathered
        return step(queries, keys, values, band_table, windows, out_weight)

    return jax.shard_map(
        local,
        mesh=mesh,
        in_specs=(
            P(("clip", "tm"), None, ("head", "sub")),
            P(("clip", "tm"), None, ("head", "sub")),
            P(("clip", "tm"), None, ("head", "sub")),
            P(),
            P(),
            P(("head", "sub"), None),
        ),
        out_specs=P(("clip", "tm"), ("head", "sub"), None),
        check_vma=False,
    )
```

```python
import functools

import jax
import jax.numpy as jnp
from jax import lax
from jax.experimental import pallas as pl
from jax.experimental.pallas import tpu as pltpu
from jax.sharding import PartitionSpec as P

HEAD = 128
ANY = pl.BlockSpec(memory_space=pl.ANY)
VMEM = pl.BlockSpec(memory_space=pltpu.VMEM)
SMEM = pl.BlockSpec(memory_space=pltpu.SMEM)
CHUNKS = 2


def gathered(queries, keys, values, band_table, windows, out_weight):
    frames, length, width = queries.shape
    heads = width // HEAD
    scale = HEAD ** (-0.5)
    here = lax.axis_index("tm") * frames
    query = queries[0].reshape(length, heads, HEAD)
    places = lax.iota(jnp.int32, length)
    gap = jnp.abs(places[:, None] - places[None, :])

    def absorb(carry, key_frame, value_frame, frame):
        peak, total, numer = carry
        reach = windows[band_table[here, frame]]
        allowed = (gap <= reach)[None]
        scores = (
            jnp.einsum(
                "phd,qhd->hpq",
                query,
                key_frame.reshape(length, heads, HEAD),
                preferred_element_type=jnp.float32,
            )
            * scale
        )
        masked = jnp.where(allowed, scores, jnp.float32(-1e30))
        top = jnp.maximum(peak, jnp.max(masked, axis=-1))
        weights = jnp.where(allowed, jnp.exp(scores - top[:, :, None]), jnp.float32(0.0))
        shrink = jnp.exp(peak - top)
        total = total * shrink + jnp.sum(weights, axis=-1)
        added = jnp.einsum(
            "hpq,qhd->phd",
            weights.astype(jnp.bfloat16),
            value_frame.reshape(length, heads, HEAD),
            preferred_element_type=jnp.float32,
        )
        numer = numer * jnp.transpose(shrink)[:, :, None] + added
        return (top, total, numer)

    carry = (
        jnp.full((heads, length), -1e30, jnp.float32),
        jnp.zeros((heads, length), jnp.float32),
        jnp.zeros((length, heads, HEAD), jnp.float32),
    )
    key_part = lax.all_gather(keys, "tm", axis=0, tiled=True)
    value_part = lax.all_gather(values, "tm", axis=0, tiled=True)

    def advance(inner, item):
        return (absorb(inner, *item), None)

    state, _ = lax.scan(
        advance, carry, (key_part, value_part, lax.iota(jnp.int32, key_part.shape[0]))
    )
    _, total, numer = state
    attended = (
        (numer / jnp.transpose(total)[:, :, None]).astype(jnp.bfloat16).reshape(length, width)
    )
    mixed = lax.psum_scatter(
        jnp.dot(attended, out_weight, preferred_element_type=jnp.float32).astype(jnp.bfloat16),
        ("head", "sub"),
        scatter_dimension=0,
        tiled=True,
    )
    return mixed[None]


def run_copies(copies, sem):
    started = [pltpu.make_async_copy(s, d, sem.at[i]) for i, (s, d) in enumerate(copies)]
    for copy in started:
        copy.start()
    for copy in started:
        copy.wait()


def pack_kernel(n, cores, tokens, q_ref, k_ref, v_ref, *rest):
    kv_out, q_out, sem = rest[:n], rest[n : 2 * n], rest[2 * n]
    z = lax.axis_index("tm")
    wide = kv_out[0].shape[2]
    half = kv_out[0].shape[1]
    copies = []
    for r in range(n):
        t = z ^ r
        cols = pl.ds(pl.multiple_of((t // cores) * wide, wide), wide)
        b = t % cores
        rows = pl.ds(pl.multiple_of(b * half, half), half)
        copies.append((k_ref.at[0, rows, cols], kv_out[r].at[0]))
        copies.append((v_ref.at[0, rows, cols], kv_out[r].at[1]))
        for x in range(half // tokens):
            place = pl.ds(pl.multiple_of((x * cores + b) * tokens, tokens), tokens)
            copies.append((q_ref.at[0, place, cols], q_out[r].at[pl.ds(x * tokens, tokens)]))
    run_copies(copies, sem)


def bias_kernel(n, cores, tokens, band_ref, reach_ref, _, bias_ref):
    z, c = lax.axis_index("tm"), lax.axis_index("sub")
    length = bias_ref.shape[1] // n
    half = length // cores
    t = (z % (n // cores)) * cores + c
    row = lax.broadcasted_iota(jnp.int32, (half, length), 0)
    key = lax.broadcasted_iota(jnp.int32, (half, length), 1)
    place = (row // tokens * cores + c) * tokens + row % tokens
    key_place = jnp.where(key < half, key + c * half, key - half + (1 - c) * half)
    gap = jnp.abs(place - key_place)
    for r in range(n):
        for s in range(n):
            reach = reach_ref[band_ref[t ^ r, t ^ s]]
            bias_ref[r * half : (r + 1) * half, s * length : (s + 1) * length] = jnp.where(
                gap <= reach, jnp.float32(0.0), jnp.float32(-1e30)
            )


def attend_kernel(n, cores, tokens, first, count, bias_ref, *rest):
    own, other, query = rest[:n], rest[n : 2 * n], rest[2 * n : 3 * n]
    outs = rest[3 * n : 4 * n]
    s_all, p_all, t_all, o_all, sem = rest[4 * n :]
    z, c = lax.axis_index("tm"), lax.axis_index("sub")
    half = own[0].shape[1]
    heads = own[0].shape[2] // HEAD
    length = half * cores
    blocks = half // tokens
    rows = blocks * count
    t = (z % (n // cores)) * cores + c
    rate = jnp.float32(HEAD ** (-0.5) * 1.4426950408889634)
    places = [
        (r, x, (r * blocks + x) * count) for r in range(n) for x in range(blocks)
    ]
    for h in range(heads):
        cols = slice(h * HEAD, (h + 1) * HEAD)
        slot = h % 2
        q = jnp.concatenate(
            [query[r][x * tokens + first : x * tokens + first + count, cols] for r, x, _ in places]
        )
        for s in range(n):
            k = jnp.concatenate([own[s][0, :, cols], other[s ^ 1][0, :, cols]])
            s_all[slot, :, s * length : (s + 1) * length] = lax.dot_general(
                q, k, (((1,), (1,)), ((), ())), preferred_element_type=jnp.float32
            )
        for r, x, at in places:
            base = r * half + x * tokens + first
            for step in range(0, count, 16):
                lines = slice(at + step, at + step + 16)
                parts = [
                    s_all[slot, lines, g : g + 128]
                    + bias_ref[base + step : base + step + 16, g : g + 128]
                    for g in range(0, n * length, 128)
                ]
                top = jnp.max(functools.reduce(jnp.maximum, parts), axis=1, keepdims=True)
                weights = [jnp.exp2((part - top) * rate) for part in parts]
                total = jnp.sum(functools.reduce(jnp.add, weights), axis=1, keepdims=True)
                t_all[slot, lines, :] = jnp.broadcast_to(1.0 / total, (16, HEAD))
                for g, weight in enumerate(weights):
                    p_all[slot, lines, g * 128 : (g + 1) * 128] = weight.astype(jnp.bfloat16)
        numer = 0.0
        for s in range(n):
            v = jnp.concatenate([own[s][1, :, cols], other[s ^ 1][1, :, cols]])
            numer += jnp.dot(
                p_all[slot, :, s * length : (s + 1) * length], v,
                preferred_element_type=jnp.float32,
            )
        result = (numer * t_all[slot]).astype(jnp.bfloat16)
        for r in range(n):
            o_all[r, :, cols] = result[r * rows : (r + 1) * rows]
    run_copies([(o_all.at[t ^ z ^ k], outs[k]) for k in range(n)], sem)


def project_kernel(n, cores, own_w, other_w, *rest):
    parts = rest[:n]
    keep_ref, send_ref, a_all, sem = rest[n:]
    z, c, x = lax.axis_index("tm"), lax.axis_index("sub"), lax.axis_index("head")
    count = keep_ref.shape[0]
    copies = []
    for k in range(n):
        for b in range(2):
            at = pl.ds(pl.multiple_of((b ^ 1 ^ x) * count, count), count)
            copies.append((parts[k].at[at], a_all.at[z ^ k, pl.ds(b * count, count)]))
    run_copies(copies, sem)
    per = n // cores
    wide = a_all.shape[2]
    total = 0.0
    for w_ref, core in ((own_w, c), (other_w, 1 - c)):
        for g in range(per):
            total += jnp.dot(
                a_all[core * per + g], w_ref[g * wide : (g + 1) * wide, :],
                preferred_element_type=jnp.float32,
            )
    send_ref[...] = total[:count].astype(send_ref.dtype)
    keep_ref[...] = total[count:]


def add_kernel(chunks, *refs):
    out_ref = refs[-1]
    for a in range(chunks):
        keep, got = refs[2 * a], refs[2 * a + 1]
        count = keep.shape[0]
        out_ref[0, a * count : (a + 1) * count] = (
            keep[...] + got[...].astype(jnp.float32)
        ).astype(out_ref.dtype)


def swapped(x, axis):
    return lax.ppermute(x, axis, [(0, 1), (1, 0)])


def spread(n, cores, queries, keys, values, band_table, windows, out_weight):
    _, length, width = queries.shape
    depth, model = out_weight.shape
    wide = width * cores // n
    half = length // cores
    tokens = half // 2
    bf16 = queries.dtype

    packed = pl.pallas_call(
        functools.partial(pack_kernel, n, cores, tokens),
        out_shape=[jax.ShapeDtypeStruct((2, half, wide), bf16)] * n
        + [jax.ShapeDtypeStruct((half, wide), bf16)] * n,
        in_specs=[ANY] * 3,
        out_specs=[VMEM] * (2 * n),
        scratch_shapes=[pltpu.SemaphoreType.DMA((4 * n,))],
        compiler_params=pltpu.CompilerParams(vmem_limit_bytes=4 * 2**20),
        name="pack",
    )(queries, keys, values)

    per = n // cores
    rounds = [
        [
            (z * cores + c, (c * per + (z ^ r) // cores) * cores + (z ^ r) % cores)
            for z in range(n)
            for c in range(cores)
        ]
        for r in range(n)
    ]
    own = [lax.ppermute(packed[r], ("tm", "sub"), rounds[r]) for r in range(n)]
    query = []
    for r in range(n):
        block, _ = lax.optimization_barrier((packed[n + r], own[(r + 1) // 2]))
        query.append(lax.ppermute(block, ("tm", "sub"), rounds[r]))
    other = [swapped(block, "sub") for block in own]

    weight, _ = lax.optimization_barrier((out_weight, own[1]))
    other_weight = swapped(weight, "sub")
    bias = pl.pallas_call(
        functools.partial(bias_kernel, n, cores, tokens),
        out_shape=jax.ShapeDtypeStruct((n * half, n * length), jnp.float32),
        in_specs=[SMEM, SMEM, ANY],
        out_specs=VMEM,
        compiler_params=pltpu.CompilerParams(vmem_limit_bytes=4 * 2**20),
        name="bias",
    )(band_table, windows, packed[0])

    count = tokens // CHUNKS
    rows = 2 * count
    sums = []
    for a in range(CHUNKS):
        outs = pl.pallas_call(
            functools.partial(attend_kernel, n, cores, tokens, a * count, count),
            out_shape=[jax.ShapeDtypeStruct((rows, wide), bf16)] * n,
            in_specs=[VMEM] * (1 + 3 * n),
            out_specs=[VMEM] * n,
            scratch_shapes=[
                pltpu.VMEM((2, n * rows, n * length), jnp.float32),
                pltpu.VMEM((2, n * rows, n * length), bf16),
                pltpu.VMEM((2, n * rows, HEAD), jnp.float32),
                pltpu.VMEM((n, rows, wide), bf16),
                pltpu.SemaphoreType.DMA((n,)),
            ],
            compiler_params=pltpu.CompilerParams(vmem_limit_bytes=24 * 2**20),
            name="attend",
        )(bias, *own, *other, *query)
        parts = [outs[0]] + [
            lax.ppermute(outs[k], "tm", [(z, z ^ k) for z in range(n)]) for k in range(1, n)
        ]
        keep, send = pl.pallas_call(
            functools.partial(project_kernel, n, cores),
            out_shape=[
                jax.ShapeDtypeStruct((count, model), jnp.float32),
                jax.ShapeDtypeStruct((count, model), bf16),
            ],
            in_specs=[VMEM] * (2 + n),
            out_specs=[VMEM] * 2,
            scratch_shapes=[
                pltpu.VMEM((n, rows, wide), bf16),
                pltpu.SemaphoreType.DMA((2 * n,)),
            ],
            compiler_params=pltpu.CompilerParams(vmem_limit_bytes=24 * 2**20),
            name="project",
        )(out_weight, other_weight, *parts)
        sums += [keep, swapped(send, "head")]
    return pl.pallas_call(
        functools.partial(add_kernel, CHUNKS),
        out_shape=jax.ShapeDtypeStruct((1, tokens, model), bf16),
        in_specs=[VMEM] * (2 * CHUNKS),
        out_specs=VMEM,
        compiler_params=pltpu.CompilerParams(vmem_limit_bytes=4 * 2**20),
        name="add",
    )(*sums)


def solution(mesh):
    n, cores, xs = mesh.shape["tm"], mesh.shape["sub"], mesh.shape["head"]

    def local(queries, keys, values, band_table, windows, out_weight):
        frames, length, width = queries.shape
        fits = (
            frames == 1
            and n & (n - 1) == 0
            and cores == 2
            and xs == 2
            and n % cores == 0
            and width * cores % (n * HEAD) == 0
            and length % (xs * cores * CHUNKS * 16) == 0
        )
        step = functools.partial(spread, n, cores) if fits else gathered
        return step(queries, keys, values, band_table, windows, out_weight)

    return jax.shard_map(
        local,
        mesh=mesh,
        in_specs=(
            P(("clip", "tm"), None, ("head", "sub")),
            P(("clip", "tm"), None, ("head", "sub")),
            P(("clip", "tm"), None, ("head", "sub")),
            P(),
            P(),
            P(("head", "sub"), None),
        ),
        out_specs=P(("clip", "tm"), ("head", "sub"), None),
        check_vma=False,
    )
```

```python
import functools

import jax
import jax.numpy as jnp
from jax import lax
from jax.experimental import pallas as pl
from jax.experimental.pallas import tpu as pltpu
from jax.sharding import PartitionSpec as P

HEAD = 128
ANY = pl.BlockSpec(memory_space=pl.ANY)
VMEM = pl.BlockSpec(memory_space=pltpu.VMEM)
HBM = pl.BlockSpec(memory_space=pltpu.HBM)
SMEM = pl.BlockSpec(memory_space=pltpu.SMEM)
CHUNKS = 2
PACK_MB = 59
TIE = 0
PIECES = 1


def gathered(queries, keys, values, band_table, windows, out_weight):
    frames, length, width = queries.shape
    heads = width // HEAD
    scale = HEAD ** (-0.5)
    here = lax.axis_index("tm") * frames
    query = queries[0].reshape(length, heads, HEAD)
    places = lax.iota(jnp.int32, length)
    gap = jnp.abs(places[:, None] - places[None, :])

    def absorb(carry, key_frame, value_frame, frame):
        peak, total, numer = carry
        reach = windows[band_table[here, frame]]
        allowed = (gap <= reach)[None]
        scores = (
            jnp.einsum(
                "phd,qhd->hpq",
                query,
                key_frame.reshape(length, heads, HEAD),
                preferred_element_type=jnp.float32,
            )
            * scale
        )
        masked = jnp.where(allowed, scores, jnp.float32(-1e30))
        top = jnp.maximum(peak, jnp.max(masked, axis=-1))
        weights = jnp.where(allowed, jnp.exp(scores - top[:, :, None]), jnp.float32(0.0))
        shrink = jnp.exp(peak - top)
        total = total * shrink + jnp.sum(weights, axis=-1)
        added = jnp.einsum(
            "hpq,qhd->phd",
            weights.astype(jnp.bfloat16),
            value_frame.reshape(length, heads, HEAD),
            preferred_element_type=jnp.float32,
        )
        numer = numer * jnp.transpose(shrink)[:, :, None] + added
        return (top, total, numer)

    carry = (
        jnp.full((heads, length), -1e30, jnp.float32),
        jnp.zeros((heads, length), jnp.float32),
        jnp.zeros((length, heads, HEAD), jnp.float32),
    )
    key_part = lax.all_gather(keys, "tm", axis=0, tiled=True)
    value_part = lax.all_gather(values, "tm", axis=0, tiled=True)

    def advance(inner, item):
        return (absorb(inner, *item), None)

    state, _ = lax.scan(
        advance, carry, (key_part, value_part, lax.iota(jnp.int32, key_part.shape[0]))
    )
    _, total, numer = state
    attended = (
        (numer / jnp.transpose(total)[:, :, None]).astype(jnp.bfloat16).reshape(length, width)
    )
    mixed = lax.psum_scatter(
        jnp.dot(attended, out_weight, preferred_element_type=jnp.float32).astype(jnp.bfloat16),
        ("head", "sub"),
        scatter_dimension=0,
        tiled=True,
    )
    return mixed[None]


def run_copies(copies, sem):
    started = [pltpu.make_async_copy(s, d, sem.at[i]) for i, (s, d) in enumerate(copies)]
    for copy in started:
        copy.start()
    for copy in started:
        copy.wait()


def pack_kernel(n, cores, tokens, q_ref, k_ref, v_ref, *rest):
    outs, held, sem = rest[:n], rest[n], rest[n + 1]
    z = lax.axis_index("tm")
    _, half, wide = outs[0].shape
    piece = held.shape[1] // PIECES
    run_copies(
        [
            (ref.at[0, pl.ds(p * piece, piece)], held.at[i, pl.ds(p * piece, piece)])
            for i, ref in enumerate((k_ref, v_ref, q_ref))
            for p in range(PIECES)
        ],
        sem,
    )
    for r in range(n):
        t = z ^ r
        cols = pl.ds(pl.multiple_of((t // cores) * wide, wide), wide)
        b = t % cores
        rows = pl.ds(pl.multiple_of(b * half, half), half)
        outs[r][0] = held[0, rows, cols]
        outs[r][1] = held[1, rows, cols]
        for x in range(half // tokens):
            place = pl.ds(pl.multiple_of((x * cores + b) * tokens, tokens), tokens)
            outs[r][2, x * tokens : (x + 1) * tokens] = held[2, place, cols]


def bias_kernel(n, cores, tokens, band_ref, reach_ref, bias_ref):
    z, c = lax.axis_index("tm"), lax.axis_index("sub")
    length = bias_ref.shape[1] // n
    half = length // cores
    t = (z % (n // cores)) * cores + c
    row = lax.broadcasted_iota(jnp.int32, (half, length), 0)
    key = lax.broadcasted_iota(jnp.int32, (half, length), 1)
    place = (row // tokens * cores + c) * tokens + row % tokens
    key_place = jnp.where(key < half, key + c * half, key - half + (1 - c) * half)
    gap = jnp.abs(place - key_place)
    for r in range(n):
        for s in range(n):
            reach = reach_ref[band_ref[t ^ r, t ^ s]]
            bias_ref[r * half : (r + 1) * half, s * length : (s + 1) * length] = jnp.where(
                gap <= reach, jnp.float32(0.0), jnp.float32(-1e30)
            )


def attend_kernel(n, cores, tokens, first, count, bias_ref, *rest):
    own, other, outs = rest[:n], rest[n : 2 * n], rest[2 * n : 3 * n]
    s_all, p_all, t_all, o_all = rest[3 * n :]
    z, c = lax.axis_index("tm"), lax.axis_index("sub")
    half = own[0].shape[1]
    heads = own[0].shape[2] // HEAD
    length = half * cores
    blocks = half // tokens
    rows = blocks * count
    t = (z % (n // cores)) * cores + c
    rate = jnp.float32(HEAD ** (-0.5) * 1.4426950408889634)
    places = [
        (r, x, (r * blocks + x) * count) for r in range(n) for x in range(blocks)
    ]
    for h in range(heads):
        cols = slice(h * HEAD, (h + 1) * HEAD)
        slot = h % 2
        q = jnp.concatenate(
            [own[r][2, x * tokens + first : x * tokens + first + count, cols] for r, x, _ in places]
        )
        for s in range(n):
            k = jnp.concatenate([own[s][0, :, cols], other[s ^ 1][0, :, cols]])
            s_all[slot, :, s * length : (s + 1) * length] = lax.dot_general(
                q, k, (((1,), (1,)), ((), ())), preferred_element_type=jnp.float32
            )
        for r, x, at in places:
            base = r * half + x * tokens + first
            for step in range(0, count, 16):
                lines = slice(at + step, at + step + 16)
                parts = [
                    s_all[slot, lines, g : g + 128]
                    + bias_ref[base + step : base + step + 16, g : g + 128]
                    for g in range(0, n * length, 128)
                ]
                top = jnp.max(functools.reduce(jnp.maximum, parts), axis=1, keepdims=True)
                weights = [jnp.exp2((part - top) * rate) for part in parts]
                total = jnp.sum(functools.reduce(jnp.add, weights), axis=1, keepdims=True)
                t_all[slot, lines, :] = jnp.broadcast_to(1.0 / total, (16, HEAD))
                for g, weight in enumerate(weights):
                    p_all[slot, lines, g * 128 : (g + 1) * 128] = weight.astype(jnp.bfloat16)
        numer = 0.0
        for s in range(n):
            v = jnp.concatenate([own[s][1, :, cols], other[s ^ 1][1, :, cols]])
            numer += jnp.dot(
                p_all[slot, :, s * length : (s + 1) * length], v,
                preferred_element_type=jnp.float32,
            )
        result = (numer * t_all[slot]).astype(jnp.bfloat16)
        for r in range(n):
            o_all[r, :, cols] = result[r * rows : (r + 1) * rows]
    for k in range(n):
        outs[k][...] = o_all[t ^ z ^ k]


def project_kernel(n, cores, own_w, other_w, *rest):
    parts = rest[:n]
    keep_ref, send_ref, a_all = rest[n:]
    z, c, x = lax.axis_index("tm"), lax.axis_index("sub"), lax.axis_index("head")
    count = keep_ref.shape[0]
    for k in range(n):
        for b in range(2):
            at = pl.ds(pl.multiple_of((b ^ 1 ^ x) * count, count), count)
            a_all[z ^ k, b * count : (b + 1) * count] = parts[k][at, :]
    per = n // cores
    wide = a_all.shape[2]
    total = 0.0
    for w_ref, core in ((own_w, c), (other_w, 1 - c)):
        for g in range(per):
            total += jnp.dot(
                a_all[core * per + g], w_ref[g * wide : (g + 1) * wide, :],
                preferred_element_type=jnp.float32,
            )
    send_ref[...] = total[:count].astype(send_ref.dtype)
    keep_ref[...] = total[count:]


def add_kernel(chunks, *refs):
    out_ref = refs[-1]
    for a in range(chunks):
        keep, got = refs[2 * a], refs[2 * a + 1]
        count = keep.shape[0]
        out_ref[0, a * count : (a + 1) * count] = (
            keep[...] + got[...].astype(jnp.float32)
        ).astype(out_ref.dtype)


def swapped(x, axis):
    return lax.ppermute(x, axis, [(0, 1), (1, 0)])


def spread(n, cores, queries, keys, values, band_table, windows, out_weight):
    _, length, width = queries.shape
    depth, model = out_weight.shape
    wide = width * cores // n
    half = length // cores
    tokens = half // 2
    count = tokens // CHUNKS
    rows = 2 * count
    bf16 = queries.dtype

    packed = pl.pallas_call(
        functools.partial(pack_kernel, n, cores, tokens),
        out_shape=[jax.ShapeDtypeStruct((3, half, wide), bf16)] * n,
        in_specs=[ANY] * 3,
        out_specs=[VMEM] * n,
        scratch_shapes=[
            pltpu.VMEM((3, length, width), bf16),
            pltpu.SemaphoreType.DMA((3 * PIECES,)),
        ],
        compiler_params=pltpu.CompilerParams(vmem_limit_bytes=PACK_MB * 2**20),
        name="pack",
    )(queries, keys, values)

    per = n // cores
    rounds = [
        [
            (z * cores + c, (c * per + (z ^ r) // cores) * cores + (z ^ r) % cores)
            for z in range(n)
            for c in range(cores)
        ]
        for r in range(n)
    ]
    bias = pl.pallas_call(
        functools.partial(bias_kernel, n, cores, tokens),
        out_shape=jax.ShapeDtypeStruct((n * half, n * length), jnp.float32),
        in_specs=[SMEM, SMEM],
        out_specs=VMEM,
        compiler_params=pltpu.CompilerParams(vmem_limit_bytes=4 * 2**20),
        name="bias",
    )(band_table, windows)
    blocks = list(packed)
    blocks[TIE], _ = lax.optimization_barrier((packed[TIE], bias))
    own = [lax.ppermute(blocks[r], ("tm", "sub"), rounds[r]) for r in range(n)]
    weight, _ = lax.optimization_barrier((out_weight, packed[0]))
    other_weight = swapped(weight, "sub")
    other = []
    for r in range(n):
        other.append(swapped(own[r], "sub"))
    bias, other_weight = lax.optimization_barrier((bias, other_weight))

    sums = []
    for a in range(CHUNKS):
        outs = pl.pallas_call(
            functools.partial(attend_kernel, n, cores, tokens, a * count, count),
            out_shape=[jax.ShapeDtypeStruct((rows, wide), bf16)] * n,
            in_specs=[VMEM] * (1 + 2 * n),
            out_specs=[VMEM] * n,
            scratch_shapes=[
                pltpu.VMEM((2, n * rows, n * length), jnp.float32),
                pltpu.VMEM((2, n * rows, n * length), bf16),
                pltpu.VMEM((2, n * rows, HEAD), jnp.float32),
                pltpu.VMEM((n, rows, wide), bf16),
            ],
            compiler_params=pltpu.CompilerParams(vmem_limit_bytes=24 * 2**20),
            name="attend",
        )(bias, *own, *other)
        parts = [outs[0]] + [
            lax.ppermute(outs[k], "tm", [(z, z ^ k) for z in range(n)]) for k in range(1, n)
        ]
        keep, send = pl.pallas_call(
            functools.partial(project_kernel, n, cores),
            out_shape=[
                jax.ShapeDtypeStruct((count, model), jnp.float32),
                jax.ShapeDtypeStruct((count, model), bf16),
            ],
            in_specs=[VMEM] * (2 + n),
            out_specs=[VMEM] * 2,
            scratch_shapes=[pltpu.VMEM((n, rows, wide), bf16)],
            compiler_params=pltpu.CompilerParams(vmem_limit_bytes=24 * 2**20),
            name="project",
        )(out_weight, other_weight, *parts)
        sums += [keep, swapped(send, "head")]
    return pl.pallas_call(
        functools.partial(add_kernel, CHUNKS),
        out_shape=jax.ShapeDtypeStruct((1, tokens, model), bf16),
        in_specs=[VMEM] * (2 * CHUNKS),
        out_specs=VMEM,
        compiler_params=pltpu.CompilerParams(vmem_limit_bytes=4 * 2**20),
        name="add",
    )(*sums)


def solution(mesh):
    n, cores, xs = mesh.shape["tm"], mesh.shape["sub"], mesh.shape["head"]

    def local(queries, keys, values, band_table, windows, out_weight):
        frames, length, width = queries.shape
        fits = (
            frames == 1
            and n & (n - 1) == 0
            and cores == 2
            and xs == 2
            and n % cores == 0
            and width * cores % (n * HEAD) == 0
            and length % (xs * cores * CHUNKS * 16) == 0
        )
        step = functools.partial(spread, n, cores) if fits else gathered
        return step(queries, keys, values, band_table, windows, out_weight)

    return jax.shard_map(
        local,
        mesh=mesh,
        in_specs=(
            P(("clip", "tm"), None, ("head", "sub")),
            P(("clip", "tm"), None, ("head", "sub")),
            P(("clip", "tm"), None, ("head", "sub")),
            P(),
            P(),
            P(("head", "sub"), None),
        ),
        out_specs=P(("clip", "tm"), ("head", "sub"), None),
        check_vma=False,
    )
```

```python
import functools

import jax
import jax.numpy as jnp
from jax import lax
from jax.experimental import pallas as pl
from jax.experimental.pallas import tpu as pltpu
from jax.sharding import PartitionSpec as P

HEAD = 128
ANY = pl.BlockSpec(memory_space=pl.ANY)
VMEM = pl.BlockSpec(memory_space=pltpu.VMEM)
HBM = pl.BlockSpec(memory_space=pltpu.HBM)
SMEM = pl.BlockSpec(memory_space=pltpu.SMEM)
CHUNKS = 2
ACROSS = 64
PACK_MB = 59
TIE = 0
FIRST = [1]
W_AFTER = 1


def gathered(queries, keys, values, band_table, windows, out_weight):
    frames, length, width = queries.shape
    heads = width // HEAD
    scale = HEAD ** (-0.5)
    here = lax.axis_index("tm") * frames
    query = queries[0].reshape(length, heads, HEAD)
    places = lax.iota(jnp.int32, length)
    gap = jnp.abs(places[:, None] - places[None, :])

    def absorb(carry, key_frame, value_frame, frame):
        peak, total, numer = carry
        reach = windows[band_table[here, frame]]
        allowed = (gap <= reach)[None]
        scores = (
            jnp.einsum(
                "phd,qhd->hpq",
                query,
                key_frame.reshape(length, heads, HEAD),
                preferred_element_type=jnp.float32,
            )
            * scale
        )
        masked = jnp.where(allowed, scores, jnp.float32(-1e30))
        top = jnp.maximum(peak, jnp.max(masked, axis=-1))
        weights = jnp.where(allowed, jnp.exp(scores - top[:, :, None]), jnp.float32(0.0))
        shrink = jnp.exp(peak - top)
        total = total * shrink + jnp.sum(weights, axis=-1)
        added = jnp.einsum(
            "hpq,qhd->phd",
            weights.astype(jnp.bfloat16),
            value_frame.reshape(length, heads, HEAD),
            preferred_element_type=jnp.float32,
        )
        numer = numer * jnp.transpose(shrink)[:, :, None] + added
        return (top, total, numer)

    carry = (
        jnp.full((heads, length), -1e30, jnp.float32),
        jnp.zeros((heads, length), jnp.float32),
        jnp.zeros((length, heads, HEAD), jnp.float32),
    )
    key_part = lax.all_gather(keys, "tm", axis=0, tiled=True)
    value_part = lax.all_gather(values, "tm", axis=0, tiled=True)

    def advance(inner, item):
        return (absorb(inner, *item), None)

    state, _ = lax.scan(
        advance, carry, (key_part, value_part, lax.iota(jnp.int32, key_part.shape[0]))
    )
    _, total, numer = state
    attended = (
        (numer / jnp.transpose(total)[:, :, None]).astype(jnp.bfloat16).reshape(length, width)
    )
    mixed = lax.psum_scatter(
        jnp.dot(attended, out_weight, preferred_element_type=jnp.float32).astype(jnp.bfloat16),
        ("head", "sub"),
        scatter_dimension=0,
        tiled=True,
    )
    return mixed[None]


def run_copies(copies, sem):
    started = [pltpu.make_async_copy(s, d, sem.at[i]) for i, (s, d) in enumerate(copies)]
    for copy in started:
        copy.start()
    for copy in started:
        copy.wait()


def pack_kernel(n, cores, tokens, rounds, q_ref, k_ref, v_ref, *rest):
    outs, sem = rest[: len(rounds)], rest[len(rounds)]
    z = lax.axis_index("tm")
    _, half, wide = outs[0].shape
    copies = []
    for r, out in zip(rounds, outs):
        t = z ^ r
        cols = pl.ds(pl.multiple_of((t // cores) * wide, wide), wide)
        b = t % cores
        rows = pl.ds(pl.multiple_of(b * half, half), half)
        copies.append((k_ref.at[0, rows, cols], out.at[0]))
        copies.append((v_ref.at[0, rows, cols], out.at[1]))
        for i in range(half // tokens):
            place = pl.ds(pl.multiple_of(((i ^ b) * cores + b) * tokens, tokens), tokens)
            copies.append((q_ref.at[0, place, cols], out.at[2, pl.ds(i * tokens, tokens)]))
    run_copies(copies, sem)


def bias_kernel(n, cores, tokens, band_ref, reach_ref, bias_ref):
    z, c = lax.axis_index("tm"), lax.axis_index("sub")
    length = bias_ref.shape[1] // n
    half = length // cores
    t = (z % (n // cores)) * cores + c
    row = lax.broadcasted_iota(jnp.int32, (half, length), 0)
    key = lax.broadcasted_iota(jnp.int32, (half, length), 1)
    place = ((row // tokens ^ c) * cores + c) * tokens + row % tokens
    key_place = jnp.where(key < half, key + c * half, key - half + (1 - c) * half)
    gap = jnp.abs(place - key_place)
    for r in range(n):
        for s in range(n):
            reach = reach_ref[band_ref[t ^ r, t ^ s]]
            bias_ref[r * half : (r + 1) * half, s * length : (s + 1) * length] = jnp.where(
                gap <= reach, jnp.float32(0.0), jnp.float32(-1e30)
            )


def attend_kernel(n, cores, tokens, first, count, bias_ref, *rest):
    own, other, outs = rest[:n], rest[n : 2 * n], rest[2 * n : 3 * n]
    s_all, p_all, o_all = rest[3 * n :]
    z, c = lax.axis_index("tm"), lax.axis_index("sub")
    half = own[0].shape[1]
    heads = own[0].shape[2] // HEAD
    length = half * cores
    blocks = half // tokens
    rows = blocks * count
    t = (z % (n // cores)) * cores + c
    rate = jnp.float32(HEAD ** (-0.5) * 1.4426950408889634)
    places = [
        (r, x, (r * blocks + x) * count) for r in range(n) for x in range(blocks)
    ]
    narrow = tokens >= ACROSS

    def hidden(r, x, s, g):
        return narrow and x == 0 and r != s and g >= half

    keyed = [(s, g) for s in range(n) for g in range(0, length, 128)]
    for slot in range(2):
        for r, x, at in places:
            for s, g in keyed:
                if hidden(r, x, s, g):
                    p_all[slot, at : at + count, s * length + g : s * length + g + 128] = (
                        jnp.zeros((count, 128), jnp.bfloat16)
                    )
    ones = jnp.ones((length, HEAD), jnp.bfloat16)
    for h in range(heads):
        cols = slice(h * HEAD, (h + 1) * HEAD)
        slot = h % 2
        q = jnp.concatenate(
            [own[r][2, x * tokens + first : x * tokens + first + count, cols] for r, x, _ in places]
        )
        for s in range(n):
            k = jnp.concatenate([own[s][0, :, cols], other[s ^ 1][0, :, cols]])
            s_all[slot, :, s * length : (s + 1) * length] = lax.dot_general(
                q, k, (((1,), (1,)), ((), ())), preferred_element_type=jnp.float32
            )
        for r, x, at in places:
            base = r * half + x * tokens + first
            used = [s * length + g for s, g in keyed if not hidden(r, x, s, g)]
            for step in range(0, count, 16):
                lines = slice(at + step, at + step + 16)
                parts = [
                    s_all[slot, lines, g : g + 128]
                    + bias_ref[base + step : base + step + 16, g : g + 128]
                    for g in used
                ]
                top = jnp.max(functools.reduce(jnp.maximum, parts), axis=1, keepdims=True)
                for g, part in zip(used, parts):
                    p_all[slot, lines, g : g + 128] = jnp.exp2((part - top) * rate).astype(
                        jnp.bfloat16
                    )
        numer = 0.0
        for s in range(n):
            v = jnp.concatenate([own[s][1, :, cols], other[s ^ 1][1, :, cols]])
            numer += jnp.dot(
                p_all[slot, :, s * length : (s + 1) * length],
                jnp.concatenate([v, ones], axis=1),
                preferred_element_type=jnp.float32,
            )
        result = (numer[:, :HEAD] / numer[:, HEAD:]).astype(jnp.bfloat16)
        for r in range(n):
            o_all[r, :, cols] = result[r * rows : (r + 1) * rows]
    for k in range(n):
        outs[n - 1 - k][...] = o_all[t ^ z ^ k]


def project_kernel(n, cores, own_w, other_w, *rest):
    parts = rest[:n]
    keep_ref, send_ref, a_all = rest[n:]
    z, c, x = lax.axis_index("tm"), lax.axis_index("sub"), lax.axis_index("head")
    count = keep_ref.shape[0]
    for k in range(n):
        for b in range(2):
            at = pl.ds(pl.multiple_of((b ^ 1 ^ x ^ c) * count, count), count)
            a_all[z ^ k, b * count : (b + 1) * count] = parts[n - 1 - k][at, :]
    per = n // cores
    wide = a_all.shape[2]
    total = 0.0
    for w_ref, core in ((own_w, c), (other_w, 1 - c)):
        for g in range(per):
            total += jnp.dot(
                a_all[core * per + g], w_ref[g * wide : (g + 1) * wide, :],
                preferred_element_type=jnp.float32,
            )
    send_ref[...] = total[:count].astype(send_ref.dtype)
    keep_ref[...] = total[count:]


def add_kernel(chunks, *refs):
    out_ref = refs[-1]
    for a in range(chunks):
        keep, got = refs[2 * a], refs[2 * a + 1]
        count = keep.shape[0]
        out_ref[0, a * count : (a + 1) * count] = (
            keep[...] + got[...].astype(jnp.float32)
        ).astype(out_ref.dtype)


def swapped(x, axis):
    return lax.ppermute(x, axis, [(0, 1), (1, 0)])


def spread(n, cores, queries, keys, values, band_table, windows, out_weight):
    _, length, width = queries.shape
    depth, model = out_weight.shape
    wide = width * cores // n
    half = length // cores
    tokens = half // 2
    count = tokens // CHUNKS
    rows = 2 * count
    bf16 = queries.dtype

    def pack(rounds):
        return pl.pallas_call(
            functools.partial(pack_kernel, n, cores, tokens, rounds),
            out_shape=[jax.ShapeDtypeStruct((3, half, wide), bf16)] * len(rounds),
            in_specs=[ANY] * 3,
            out_specs=[VMEM] * len(rounds),
            scratch_shapes=[pltpu.SemaphoreType.DMA((4 * len(rounds),))],
            compiler_params=pltpu.CompilerParams(vmem_limit_bytes=PACK_MB * 2**20),
            name="pack",
        )(queries, keys, values)

    packed = dict(zip(FIRST, pack(FIRST)))
    others = [r for r in range(n) if r not in FIRST]
    packed.update(zip(others, pack(others)))
    per = n // cores
    rounds = [
        [
            (z * cores + c, (c * per + (z ^ r) // cores) * cores + (z ^ r) % cores)
            for z in range(n)
            for c in range(cores)
        ]
        for r in range(n)
    ]
    bias = pl.pallas_call(
        functools.partial(bias_kernel, n, cores, tokens),
        out_shape=jax.ShapeDtypeStruct((n * half, n * length), jnp.float32),
        in_specs=[SMEM, SMEM],
        out_specs=VMEM,
        compiler_params=pltpu.CompilerParams(vmem_limit_bytes=4 * 2**20),
        name="bias",
    )(band_table, windows)
    blocks = [packed[r] for r in range(n)]
    blocks[TIE], _ = lax.optimization_barrier((packed[TIE], bias))
    own = [lax.ppermute(blocks[r], ("tm", "sub"), rounds[r]) for r in range(n)]
    weight, _ = lax.optimization_barrier((out_weight, packed[W_AFTER]))
    other_weight = swapped(weight, "sub")
    other = []
    for r in range(n):
        other.append(swapped(own[r], "sub"))
    bias, other_weight = lax.optimization_barrier((bias, other_weight))

    sums = []
    for a in range(CHUNKS):
        outs = pl.pallas_call(
            functools.partial(attend_kernel, n, cores, tokens, a * count, count),
            out_shape=[jax.ShapeDtypeStruct((rows, wide), bf16)] * n,
            in_specs=[VMEM] * (1 + 2 * n),
            out_specs=[VMEM] * n,
            scratch_shapes=[
                pltpu.VMEM((2, n * rows, n * length), jnp.float32),
                pltpu.VMEM((2, n * rows, n * length), bf16),
                pltpu.VMEM((n, rows, wide), bf16),
            ],
            compiler_params=pltpu.CompilerParams(vmem_limit_bytes=24 * 2**20),
            name="attend",
        )(bias, *own, *other)
        parts = [
            lax.ppermute(outs[n - 1 - k], "tm", [(z, z ^ k) for z in range(n)])
            for k in range(n - 1, 0, -1)
        ] + [outs[n - 1]]
        keep, send = pl.pallas_call(
            functools.partial(project_kernel, n, cores),
            out_shape=[
                jax.ShapeDtypeStruct((count, model), jnp.float32),
                jax.ShapeDtypeStruct((count, model), bf16),
            ],
            in_specs=[VMEM] * (2 + n),
            out_specs=[VMEM] * 2,
            scratch_shapes=[pltpu.VMEM((n, rows, wide), bf16)],
            compiler_params=pltpu.CompilerParams(vmem_limit_bytes=24 * 2**20),
            name="project",
        )(out_weight, other_weight, *parts)
        sums += [keep, swapped(send, "head")]
    return pl.pallas_call(
        functools.partial(add_kernel, CHUNKS),
        out_shape=jax.ShapeDtypeStruct((1, tokens, model), bf16),
        in_specs=[VMEM] * (2 * CHUNKS),
        out_specs=VMEM,
        compiler_params=pltpu.CompilerParams(vmem_limit_bytes=4 * 2**20),
        name="add",
    )(*sums)


def solution(mesh):
    n, cores, xs = mesh.shape["tm"], mesh.shape["sub"], mesh.shape["head"]

    def local(queries, keys, values, band_table, windows, out_weight):
        frames, length, width = queries.shape
        fits = (
            frames == 1
            and n & (n - 1) == 0
            and cores == 2
            and xs == 2
            and n % cores == 0
            and width * cores % (n * HEAD) == 0
            and length % (xs * cores * CHUNKS * 16) == 0
        )
        step = functools.partial(spread, n, cores) if fits else gathered
        return step(queries, keys, values, band_table, windows, out_weight)

    return jax.shard_map(
        local,
        mesh=mesh,
        in_specs=(
            P(("clip", "tm"), None, ("head", "sub")),
            P(("clip", "tm"), None, ("head", "sub")),
            P(("clip", "tm"), None, ("head", "sub")),
            P(),
            P(),
            P(("head", "sub"), None),
        ),
        out_specs=P(("clip", "tm"), ("head", "sub"), None),
        check_vma=False,
    )
```

```python
import functools

import jax
import jax.numpy as jnp
from jax import lax
from jax.experimental import pallas as pl
from jax.experimental.pallas import tpu as pltpu
from jax.sharding import PartitionSpec as P

HEAD = 128
ANY = pl.BlockSpec(memory_space=pl.ANY)
VMEM = pl.BlockSpec(memory_space=pltpu.VMEM)
HBM = pl.BlockSpec(memory_space=pltpu.HBM)
SMEM = pl.BlockSpec(memory_space=pltpu.SMEM)
CHUNKS = 2
ACROSS = 64
PACK_MB = 59
TIE = 0
FIRST = [2]
W_AFTER = 2


def gathered(queries, keys, values, band_table, windows, out_weight):
    frames, length, width = queries.shape
    heads = width // HEAD
    scale = HEAD ** (-0.5)
    here = lax.axis_index("tm") * frames
    query = queries[0].reshape(length, heads, HEAD)
    places = lax.iota(jnp.int32, length)
    gap = jnp.abs(places[:, None] - places[None, :])

    def absorb(carry, key_frame, value_frame, frame):
        peak, total, numer = carry
        reach = windows[band_table[here, frame]]
        allowed = (gap <= reach)[None]
        scores = (
            jnp.einsum(
                "phd,qhd->hpq",
                query,
                key_frame.reshape(length, heads, HEAD),
                preferred_element_type=jnp.float32,
            )
            * scale
        )
        masked = jnp.where(allowed, scores, jnp.float32(-1e30))
        top = jnp.maximum(peak, jnp.max(masked, axis=-1))
        weights = jnp.where(allowed, jnp.exp(scores - top[:, :, None]), jnp.float32(0.0))
        shrink = jnp.exp(peak - top)
        total = total * shrink + jnp.sum(weights, axis=-1)
        added = jnp.einsum(
            "hpq,qhd->phd",
            weights.astype(jnp.bfloat16),
            value_frame.reshape(length, heads, HEAD),
            preferred_element_type=jnp.float32,
        )
        numer = numer * jnp.transpose(shrink)[:, :, None] + added
        return (top, total, numer)

    carry = (
        jnp.full((heads, length), -1e30, jnp.float32),
        jnp.zeros((heads, length), jnp.float32),
        jnp.zeros((length, heads, HEAD), jnp.float32),
    )
    key_part = lax.all_gather(keys, "tm", axis=0, tiled=True)
    value_part = lax.all_gather(values, "tm", axis=0, tiled=True)

    def advance(inner, item):
        return (absorb(inner, *item), None)

    state, _ = lax.scan(
        advance, carry, (key_part, value_part, lax.iota(jnp.int32, key_part.shape[0]))
    )
    _, total, numer = state
    attended = (
        (numer / jnp.transpose(total)[:, :, None]).astype(jnp.bfloat16).reshape(length, width)
    )
    mixed = lax.psum_scatter(
        jnp.dot(attended, out_weight, preferred_element_type=jnp.float32).astype(jnp.bfloat16),
        ("head", "sub"),
        scatter_dimension=0,
        tiled=True,
    )
    return mixed[None]


def run_copies(copies, sem):
    started = [pltpu.make_async_copy(s, d, sem.at[i]) for i, (s, d) in enumerate(copies)]
    for copy in started:
        copy.start()
    for copy in started:
        copy.wait()


def pack_kernel(n, cores, tokens, rounds, q_ref, k_ref, v_ref, *rest):
    outs, sem = rest[: len(rounds)], rest[len(rounds)]
    z = lax.axis_index("tm")
    _, half, wide = outs[0].shape
    copies = []
    for r, out in zip(rounds, outs):
        t = z ^ r
        cols = pl.ds(pl.multiple_of((t // cores) * wide, wide), wide)
        b = t % cores
        rows = pl.ds(pl.multiple_of(b * half, half), half)
        copies.append((k_ref.at[0, rows, cols], out.at[0]))
        copies.append((v_ref.at[0, rows, cols], out.at[1]))
        for i in range(half // tokens):
            place = pl.ds(pl.multiple_of(((i ^ b) * cores + b) * tokens, tokens), tokens)
            copies.append((q_ref.at[0, place, cols], out.at[2, pl.ds(i * tokens, tokens)]))
    run_copies(copies, sem)


def bias_kernel(n, cores, tokens, band_ref, reach_ref, bias_ref):
    z, c = lax.axis_index("tm"), lax.axis_index("sub")
    length = bias_ref.shape[1] // n
    half = length // cores
    t = (z % (n // cores)) * cores + c
    row = lax.broadcasted_iota(jnp.int32, (half, length), 0)
    key = lax.broadcasted_iota(jnp.int32, (half, length), 1)
    place = ((row // tokens ^ c) * cores + c) * tokens + row % tokens
    key_place = jnp.where(key < half, key + c * half, key - half + (1 - c) * half)
    gap = jnp.abs(place - key_place)
    for r in range(n):
        for s in range(n):
            reach = reach_ref[band_ref[t ^ r, t ^ s]]
            bias_ref[r * half : (r + 1) * half, s * length : (s + 1) * length] = jnp.where(
                gap <= reach, jnp.float32(0.0), jnp.float32(-1e30)
            )


RATE = HEAD ** (-0.5) * 1.4426950408889634
LAST = 1


def hidden(tokens, half, r, at, s, g):
    return tokens >= ACROSS and at == 0 and r != s and g >= half


def attend_early_kernel(n, cores, tokens, bias_ref, *rest):
    own, other = rest[:n], rest[n : 2 * n - 1]
    numer_ref, total_ref, top_ref, s_all, p_all = rest[2 * n - 1 :]
    half = own[0].shape[1]
    heads = own[0].shape[2] // HEAD
    length = half * cores
    rate = jnp.float32(RATE)
    keyed = [
        (s, g) for s in range(n) for g in range(0, length, 128) if s != LAST or g < half
    ]
    places = [(r, at) for r in range(n) for at in range(0, half, tokens)]

    def both(i, s, cols):
        mine = own[s][i, :, cols]
        if s == LAST:
            return mine
        return jnp.concatenate([mine, other[(s ^ 1) - 1][i, :, cols]])

    for slot in range(2):
        for r, at in places:
            for s, g in keyed:
                if hidden(tokens, half, r, at, s, g):
                    lines = slice(r * half + at, r * half + at + tokens)
                    p_all[slot, lines, s * length + g : s * length + g + 128] = jnp.zeros(
                        (tokens, 128), jnp.bfloat16
                    )

    def score(h, s):
        cols = slice(h * HEAD, (h + 1) * HEAD)
        q = jnp.concatenate([own[r][2, :, cols] for r in range(n)])
        k = both(0, s, cols)
        s_all[h % 2, :, s * length : s * length + k.shape[0]] = lax.dot_general(
            q, k, (((1,), (1,)), ((), ())), preferred_element_type=jnp.float32
        )

    def soften(h, r, at):
        used = [s * length + g for s, g in keyed if not hidden(tokens, half, r, at, s, g)]
        for step in range(r * half + at, r * half + at + tokens, 16):
            lines = slice(step, step + 16)
            parts = [
                s_all[h % 2, lines, g : g + 128] + bias_ref[lines, g : g + 128] for g in used
            ]
            top = jnp.max(functools.reduce(jnp.maximum, parts), axis=1, keepdims=True)
            top_ref[h, lines, :] = jnp.broadcast_to(top, (16, HEAD))
            for g, part in zip(used, parts):
                p_all[h % 2, lines, g : g + 128] = jnp.exp2((part - top) * rate).astype(
                    jnp.bfloat16
                )

    def mix(h, r):
        cols = slice(h * HEAD, (h + 1) * HEAD)
        numer = 0.0
        lines = slice(r * half, (r + 1) * half)
        for s in range(n):
            v = both(1, s, cols)
            numer += jnp.dot(
                p_all[h % 2, lines, s * length : s * length + v.shape[0]],
                jnp.concatenate([v, jnp.ones_like(v)], axis=1),
                preferred_element_type=jnp.float32,
            )
        numer_ref[h, lines, :] = numer[:, :HEAD]
        total_ref[h, lines, :] = numer[:, HEAD:]

    for s in range(n):
        score(0, s)
    for h in range(heads):
        for r in range(n):
            if h + 1 < heads:
                score(h + 1, r)
            for at in range(0, half, tokens):
                soften(h, r, at)
            mix(h, r)


def attend_late_kernel(n, cores, tokens, bias_ref, numer_ref, total_ref, top_ref, *rest):
    own, other, outs = rest[:n], rest[n], rest[n + 1 : -4]
    s_all, p_all, f_all, o_all = rest[-4:]
    z, c = lax.axis_index("tm"), lax.axis_index("sub")
    half = own[0].shape[1]
    heads = own[0].shape[2] // HEAD
    length = half * cores
    t = (z % (n // cores)) * cores + c
    rate = jnp.float32(RATE)
    first = LAST * length + half
    seen = [
        (r, at)
        for r in range(n)
        for at in range(0, half, tokens)
        if not hidden(tokens, half, r, at, LAST, half)
    ]

    def score(h):
        cols = slice(h * HEAD, (h + 1) * HEAD)
        q = jnp.concatenate([own[r][2, at : at + tokens, cols] for r, at in seen])
        s_all[h] = lax.dot_general(
            q, other[0, :, cols], (((1,), (1,)), ((), ())), preferred_element_type=jnp.float32
        )

    for h in range(heads):
        score(h)
    for h in range(heads):
        cols = slice(h * HEAD, (h + 1) * HEAD)
        for i, (r, at) in enumerate(seen):
            for step in range(0, tokens, 16):
                lines = slice(i * tokens + step, i * tokens + step + 16)
                place = slice(r * half + at + step, r * half + at + step + 16)
                parts = [
                    s_all[h, lines, g : g + 128] + bias_ref[place, first + g : first + g + 128]
                    for g in range(0, half, 128)
                ]
                old = top_ref[h, place, :]
                top = jnp.max(functools.reduce(jnp.maximum, parts), axis=1, keepdims=True)
                top = jnp.maximum(old, top)
                f_all[h, lines, :] = jnp.exp2((old - top) * rate)
                for g, part in zip(range(0, half, 128), parts):
                    p_all[h, lines, g : g + 128] = jnp.exp2((part - top[:, :1]) * rate).astype(
                        jnp.bfloat16
                    )
        v = other[1, :, cols]
        added = jnp.dot(
            p_all[h], jnp.concatenate([v, jnp.ones_like(v)], axis=1),
            preferred_element_type=jnp.float32,
        )
        for r in range(n):
            for at in range(0, half, tokens):
                place = slice(r * half + at, r * half + at + tokens)
                numer, total = numer_ref[h, place, :], total_ref[h, place, :]
                if (r, at) in seen:
                    i = seen.index((r, at)) * tokens
                    shrink = f_all[h, i : i + tokens, :]
                    numer = numer * shrink + added[i : i + tokens, :HEAD]
                    total = total * shrink + added[i : i + tokens, HEAD:]
                o_all[r, at : at + tokens, cols] = (numer / total).astype(jnp.bfloat16)

    count = tokens // CHUNKS
    rows = 2 * count
    for k, chunks, out in zip(*layout(n), outs):
        for i, a in enumerate(chunks):
            for b in range(2):
                out[i * rows + b * count : i * rows + (b + 1) * count, :] = o_all[
                    t ^ z ^ k, b * tokens + a * count : b * tokens + (a + 1) * count, :
                ]


def layout(n):
    order = [(k, [a]) for a in range(CHUNKS) for k in range(n - 1, -1, -1)]
    return [k for k, _ in order], [chunks for _, chunks in order]


def project_kernel(n, cores, places, own_w, other_w, *rest):
    parts = rest[:n]
    keep_ref, send_ref, a_all = rest[n:]
    z, c, x = lax.axis_index("tm"), lax.axis_index("sub"), lax.axis_index("head")
    count = keep_ref.shape[0]
    for (k, first), part in zip(places, parts):
        for b in range(2):
            at = pl.ds(pl.multiple_of((b ^ 1 ^ x ^ c) * count + first, count), count)
            a_all[z ^ k, b * count : (b + 1) * count] = part[at, :]
    per = n // cores
    wide = a_all.shape[2]
    total = 0.0
    for w_ref, core in ((own_w, c), (other_w, 1 - c)):
        for g in range(per):
            total += jnp.dot(
                a_all[core * per + g], w_ref[g * wide : (g + 1) * wide, :],
                preferred_element_type=jnp.float32,
            )
    send_ref[...] = total[:count].astype(send_ref.dtype)
    keep_ref[...] = total[count:]


def add_kernel(chunks, *refs):
    out_ref = refs[-1]
    for a in range(chunks):
        keep, got = refs[2 * a], refs[2 * a + 1]
        count = keep.shape[0]
        out_ref[0, a * count : (a + 1) * count] = (
            keep[...] + got[...].astype(jnp.float32)
        ).astype(out_ref.dtype)


def swapped(x, axis):
    return lax.ppermute(x, axis, [(0, 1), (1, 0)])


def spread(n, cores, queries, keys, values, band_table, windows, out_weight):
    _, length, width = queries.shape
    depth, model = out_weight.shape
    wide = width * cores // n
    half = length // cores
    tokens = half // 2
    count = tokens // CHUNKS
    rows = 2 * count
    bf16 = queries.dtype

    def pack(rounds, mb, queries, keys, values):
        return pl.pallas_call(
            functools.partial(pack_kernel, n, cores, tokens, rounds),
            out_shape=[jax.ShapeDtypeStruct((3, half, wide), bf16)] * len(rounds),
            in_specs=[ANY] * 3,
            out_specs=[VMEM] * len(rounds),
            scratch_shapes=[pltpu.SemaphoreType.DMA((4 * len(rounds),))],
            compiler_params=pltpu.CompilerParams(vmem_limit_bytes=mb * 2**20),
            name="pack",
        )(queries, keys, values)

    packed = dict(zip(FIRST, pack(FIRST, PACK_MB, queries, keys, values)))
    others = [r for r in range(n) if r not in FIRST]
    arrays = lax.optimization_barrier((queries, keys, values, packed[FIRST[0]]))[:3]
    packed.update(zip(others, pack(others, 6, *arrays)))
    per = n // cores
    rounds = [
        [
            (z * cores + c, (c * per + (z ^ r) // cores) * cores + (z ^ r) % cores)
            for z in range(n)
            for c in range(cores)
        ]
        for r in range(n)
    ]
    bias = pl.pallas_call(
        functools.partial(bias_kernel, n, cores, tokens),
        out_shape=jax.ShapeDtypeStruct((n * half, n * length), jnp.float32),
        in_specs=[SMEM, SMEM],
        out_specs=VMEM,
        compiler_params=pltpu.CompilerParams(vmem_limit_bytes=4 * 2**20),
        name="bias",
    )(band_table, windows)
    blocks = [packed[r] for r in range(n)]
    blocks[TIE], _ = lax.optimization_barrier((packed[TIE], bias))
    own = [lax.ppermute(blocks[r], ("tm", "sub"), rounds[r]) for r in range(n)]
    weight, _ = lax.optimization_barrier((out_weight, packed[W_AFTER]))
    other_weight = swapped(weight, "sub")
    other = []
    for r in range(n):
        other.append(swapped(own[r], "sub"))
    bias, other_weight = lax.optimization_barrier((bias, other_weight))

    travels = list(zip(*layout(n)))
    heads = wide // HEAD
    f32 = jnp.float32
    partial = pl.pallas_call(
        functools.partial(attend_early_kernel, n, cores, tokens),
        out_shape=[jax.ShapeDtypeStruct((heads, n * half, HEAD), f32)] * 3,
        in_specs=[VMEM] * (2 * n),
        out_specs=[VMEM] * 3,
        scratch_shapes=[
            pltpu.VMEM((2, n * half, n * length), f32),
            pltpu.VMEM((2, n * half, n * length), bf16),
        ],
        compiler_params=pltpu.CompilerParams(vmem_limit_bytes=24 * 2**20),
        name="attend_early",
    )(bias, *own, *other[1:])
    seen = n * half if tokens < ACROSS else n * half - (n - 1) * tokens
    outs = pl.pallas_call(
        functools.partial(attend_late_kernel, n, cores, tokens),
        out_shape=[jax.ShapeDtypeStruct((len(chunks) * rows, wide), bf16) for _, chunks in travels],
        in_specs=[VMEM] * (5 + n),
        out_specs=[VMEM] * len(travels),
        scratch_shapes=[
            pltpu.VMEM((heads, seen, half), f32),
            pltpu.VMEM((heads, seen, half), bf16),
            pltpu.VMEM((heads, seen, HEAD), f32),
            pltpu.VMEM((n, half, wide), bf16),
        ],
        compiler_params=pltpu.CompilerParams(vmem_limit_bytes=24 * 2**20),
        name="attend_late",
    )(bias, *partial, *own, other[0])
    back = [
        (k, chunks, lax.ppermute(out, "tm", [(z, z ^ k) for z in range(n)]) if k else out)
        for (k, chunks), out in zip(travels, outs)
    ]
    sums = []
    for a in range(CHUNKS):
        held = [(k, chunks.index(a) * rows, part) for k, chunks, part in back if a in chunks]
        places = [(k, first) for k, first, _ in held]
        parts = [part for _, _, part in held]
        keep, send = pl.pallas_call(
            functools.partial(project_kernel, n, cores, places),
            out_shape=[
                jax.ShapeDtypeStruct((count, model), jnp.float32),
                jax.ShapeDtypeStruct((count, model), bf16),
            ],
            in_specs=[VMEM] * (2 + n),
            out_specs=[VMEM] * 2,
            scratch_shapes=[pltpu.VMEM((n, rows, wide), bf16)],
            compiler_params=pltpu.CompilerParams(vmem_limit_bytes=24 * 2**20),
            name="project",
        )(out_weight, other_weight, *parts)
        sums += [keep, swapped(send, "head")]
    return pl.pallas_call(
        functools.partial(add_kernel, CHUNKS),
        out_shape=jax.ShapeDtypeStruct((1, tokens, model), bf16),
        in_specs=[VMEM] * (2 * CHUNKS),
        out_specs=VMEM,
        compiler_params=pltpu.CompilerParams(vmem_limit_bytes=4 * 2**20),
        name="add",
    )(*sums)


def solution(mesh):
    n, cores, xs = mesh.shape["tm"], mesh.shape["sub"], mesh.shape["head"]

    def local(queries, keys, values, band_table, windows, out_weight):
        frames, length, width = queries.shape
        fits = (
            frames == 1
            and n & (n - 1) == 0
            and cores == 2
            and xs == 2
            and n % cores == 0
            and width * cores % (n * HEAD) == 0
            and length % (xs * cores * CHUNKS * 16) == 0
        )
        step = functools.partial(spread, n, cores) if fits else gathered
        return step(queries, keys, values, band_table, windows, out_weight)

    return jax.shard_map(
        local,
        mesh=mesh,
        in_specs=(
            P(("clip", "tm"), None, ("head", "sub")),
            P(("clip", "tm"), None, ("head", "sub")),
            P(("clip", "tm"), None, ("head", "sub")),
            P(),
            P(),
            P(("head", "sub"), None),
        ),
        out_specs=P(("clip", "tm"), ("head", "sub"), None),
        check_vma=False,
    )
```

```python
import functools

import jax
import jax.numpy as jnp
from jax import lax
from jax.experimental import pallas as pl
from jax.experimental.pallas import tpu as pltpu
from jax.sharding import PartitionSpec as P

HEAD = 128
ANY = pl.BlockSpec(memory_space=pl.ANY)
VMEM = pl.BlockSpec(memory_space=pltpu.VMEM)
HBM = pl.BlockSpec(memory_space=pltpu.HBM)
SMEM = pl.BlockSpec(memory_space=pltpu.SMEM)
CHUNKS = 2
ACROSS = 64
GROUP = 1
INTERLEAVE = True
PACK_MB = 59
TIE = 0
FIRST = [2]
W_AFTER = 2


def gathered(queries, keys, values, band_table, windows, out_weight):
    frames, length, width = queries.shape
    heads = width // HEAD
    scale = HEAD ** (-0.5)
    here = lax.axis_index("tm") * frames
    query = queries[0].reshape(length, heads, HEAD)
    places = lax.iota(jnp.int32, length)
    gap = jnp.abs(places[:, None] - places[None, :])

    def absorb(carry, key_frame, value_frame, frame):
        peak, total, numer = carry
        reach = windows[band_table[here, frame]]
        allowed = (gap <= reach)[None]
        scores = (
            jnp.einsum(
                "phd,qhd->hpq",
                query,
                key_frame.reshape(length, heads, HEAD),
                preferred_element_type=jnp.float32,
            )
            * scale
        )
        masked = jnp.where(allowed, scores, jnp.float32(-1e30))
        top = jnp.maximum(peak, jnp.max(masked, axis=-1))
        weights = jnp.where(allowed, jnp.exp(scores - top[:, :, None]), jnp.float32(0.0))
        shrink = jnp.exp(peak - top)
        total = total * shrink + jnp.sum(weights, axis=-1)
        added = jnp.einsum(
            "hpq,qhd->phd",
            weights.astype(jnp.bfloat16),
            value_frame.reshape(length, heads, HEAD),
            preferred_element_type=jnp.float32,
        )
        numer = numer * jnp.transpose(shrink)[:, :, None] + added
        return (top, total, numer)

    carry = (
        jnp.full((heads, length), -1e30, jnp.float32),
        jnp.zeros((heads, length), jnp.float32),
        jnp.zeros((length, heads, HEAD), jnp.float32),
    )
    key_part = lax.all_gather(keys, "tm", axis=0, tiled=True)
    value_part = lax.all_gather(values, "tm", axis=0, tiled=True)

    def advance(inner, item):
        return (absorb(inner, *item), None)

    state, _ = lax.scan(
        advance, carry, (key_part, value_part, lax.iota(jnp.int32, key_part.shape[0]))
    )
    _, total, numer = state
    attended = (
        (numer / jnp.transpose(total)[:, :, None]).astype(jnp.bfloat16).reshape(length, width)
    )
    mixed = lax.psum_scatter(
        jnp.dot(attended, out_weight, preferred_element_type=jnp.float32).astype(jnp.bfloat16),
        ("head", "sub"),
        scatter_dimension=0,
        tiled=True,
    )
    return mixed[None]


def run_copies(copies, sem):
    started = [pltpu.make_async_copy(s, d, sem.at[i]) for i, (s, d) in enumerate(copies)]
    for copy in started:
        copy.start()
    for copy in started:
        copy.wait()


def pack_kernel(n, cores, tokens, rounds, q_ref, k_ref, v_ref, *rest):
    outs, sem = rest[: len(rounds)], rest[len(rounds)]
    z = lax.axis_index("tm")
    _, half, wide = outs[0].shape
    copies = []
    for r, out in zip(rounds, outs):
        t = z ^ r
        cols = pl.ds(pl.multiple_of((t // cores) * wide, wide), wide)
        b = t % cores
        rows = pl.ds(pl.multiple_of(b * half, half), half)
        copies.append((k_ref.at[0, rows, cols], out.at[0]))
        copies.append((v_ref.at[0, rows, cols], out.at[1]))
        for i in range(half // tokens):
            place = pl.ds(pl.multiple_of(((i ^ b) * cores + b) * tokens, tokens), tokens)
            copies.append((q_ref.at[0, place, cols], out.at[2, pl.ds(i * tokens, tokens)]))
    run_copies(copies, sem)


def bias_kernel(n, cores, tokens, band_ref, reach_ref, bias_ref):
    z, c = lax.axis_index("tm"), lax.axis_index("sub")
    length = bias_ref.shape[1] // n
    half = length // cores
    t = (z % (n // cores)) * cores + c
    row = lax.broadcasted_iota(jnp.int32, (half, length), 0)
    key = lax.broadcasted_iota(jnp.int32, (half, length), 1)
    place = ((row // tokens ^ c) * cores + c) * tokens + row % tokens
    key_place = jnp.where(key < half, key + c * half, key - half + (1 - c) * half)
    gap = jnp.abs(place - key_place)
    for r in range(n):
        for s in range(n):
            reach = reach_ref[band_ref[t ^ r, t ^ s]]
            bias_ref[r * half : (r + 1) * half, s * length : (s + 1) * length] = jnp.where(
                gap <= reach, jnp.float32(0.0), jnp.float32(-1e30)
            )


def attend_kernel(n, cores, tokens, bias_ref, *rest):
    own, other, outs = rest[:n], rest[n : 2 * n], rest[2 * n : -3]
    s_all, p_all, o_all = rest[-3:]
    z, c = lax.axis_index("tm"), lax.axis_index("sub")
    half = own[0].shape[1]
    heads = own[0].shape[2] // HEAD
    length = half * cores
    t = (z % (n // cores)) * cores + c
    rate = jnp.float32(HEAD ** (-0.5) * 1.4426950408889634)
    narrow = tokens >= ACROSS
    keyed = [(s, g) for s in range(n) for g in range(0, length, 128)]
    places = [(r, at) for r in range(n) for at in range(0, half, tokens)]

    def hidden(r, at, s, g):
        return narrow and at == 0 and r != s and g >= half

    for slot in range(2):
        for r, at in places:
            for s, g in keyed:
                if hidden(r, at, s, g):
                    lines = slice(r * half + at, r * half + at + tokens)
                    p_all[slot, lines, s * length + g : s * length + g + 128] = jnp.zeros(
                        (tokens, 128), jnp.bfloat16
                    )
    ones = jnp.ones((length, HEAD), jnp.bfloat16)

    def score(h, s):
        cols = slice(h * HEAD, (h + 1) * HEAD)
        q = jnp.concatenate([own[r][2, :, cols] for r in range(n)])
        k = jnp.concatenate([own[s][0, :, cols], other[s ^ 1][0, :, cols]])
        s_all[h % 2, :, s * length : (s + 1) * length] = lax.dot_general(
            q, k, (((1,), (1,)), ((), ())), preferred_element_type=jnp.float32
        )

    def soften(h, r, at):
        used = [s * length + g for s, g in keyed if not hidden(r, at, s, g)]
        for step in range(r * half + at, r * half + at + tokens, 16):
            lines = slice(step, step + 16)
            parts = [
                s_all[h % 2, lines, g : g + 128] + bias_ref[lines, g : g + 128] for g in used
            ]
            top = jnp.max(functools.reduce(jnp.maximum, parts), axis=1, keepdims=True)
            for g, part in zip(used, parts):
                p_all[h % 2, lines, g : g + 128] = jnp.exp2((part - top) * rate).astype(
                    jnp.bfloat16
                )

    def mix(h, r):
        cols = slice(h * HEAD, (h + 1) * HEAD)
        numer = 0.0
        lines = slice(r * half, (r + GROUP) * half)
        for s in range(n):
            v = jnp.concatenate([own[s][1, :, cols], other[s ^ 1][1, :, cols]])
            numer += jnp.dot(
                p_all[h % 2, lines, s * length : (s + 1) * length],
                jnp.concatenate([v, ones], axis=1),
                preferred_element_type=jnp.float32,
            )
        result = (numer[:, :HEAD] / numer[:, HEAD:]).astype(jnp.bfloat16)
        for i in range(GROUP):
            o_all[r + i, :, cols] = result[i * half : (i + 1) * half]

    for s in range(n):
        score(0, s)
    for h in range(heads):
        for r in range(n):
            if INTERLEAVE and h + 1 < heads:
                score(h + 1, r)
            for at in range(0, half, tokens):
                soften(h, r, at)
            if (r + 1) % GROUP == 0:
                mix(h, r + 1 - GROUP)
        if not INTERLEAVE and h + 1 < heads:
            for s in range(n):
                score(h + 1, s)

    count = tokens // CHUNKS
    rows = 2 * count
    for k, chunks, out in zip(*layout(n), outs):
        for i, a in enumerate(chunks):
            for b in range(2):
                out[i * rows + b * count : i * rows + (b + 1) * count, :] = o_all[
                    t ^ z ^ k, b * tokens + a * count : b * tokens + (a + 1) * count, :
                ]


def layout(n):
    order = [(k, [a]) for a in range(CHUNKS) for k in range(n - 1, -1, -1)]
    return [k for k, _ in order], [chunks for _, chunks in order]


def project_kernel(n, cores, places, own_w, other_w, *rest):
    parts = rest[:n]
    keep_ref, send_ref, a_all = rest[n:]
    z, c, x = lax.axis_index("tm"), lax.axis_index("sub"), lax.axis_index("head")
    count = keep_ref.shape[0]
    for (k, first), part in zip(places, parts):
        for b in range(2):
            at = pl.ds(pl.multiple_of((b ^ 1 ^ x ^ c) * count + first, count), count)
            a_all[z ^ k, b * count : (b + 1) * count] = part[at, :]
    per = n // cores
    wide = a_all.shape[2]
    total = 0.0
    for w_ref, core in ((own_w, c), (other_w, 1 - c)):
        for g in range(per):
            total += jnp.dot(
                a_all[core * per + g], w_ref[g * wide : (g + 1) * wide, :],
                preferred_element_type=jnp.float32,
            )
    send_ref[...] = total[:count].astype(send_ref.dtype)
    keep_ref[...] = total[count:]


def add_kernel(chunks, *refs):
    out_ref = refs[-1]
    for a in range(chunks):
        keep, got = refs[2 * a], refs[2 * a + 1]
        count = keep.shape[0]
        out_ref[0, a * count : (a + 1) * count] = (
            keep[...] + got[...].astype(jnp.float32)
        ).astype(out_ref.dtype)


def swapped(x, axis):
    return lax.ppermute(x, axis, [(0, 1), (1, 0)])


def spread(n, cores, queries, keys, values, band_table, windows, out_weight):
    _, length, width = queries.shape
    depth, model = out_weight.shape
    wide = width * cores // n
    half = length // cores
    tokens = half // 2
    count = tokens // CHUNKS
    rows = 2 * count
    bf16 = queries.dtype

    def pack(rounds, mb, queries, keys, values):
        return pl.pallas_call(
            functools.partial(pack_kernel, n, cores, tokens, rounds),
            out_shape=[jax.ShapeDtypeStruct((3, half, wide), bf16)] * len(rounds),
            in_specs=[ANY] * 3,
            out_specs=[VMEM] * len(rounds),
            scratch_shapes=[pltpu.SemaphoreType.DMA((4 * len(rounds),))],
            compiler_params=pltpu.CompilerParams(vmem_limit_bytes=mb * 2**20),
            name="pack",
        )(queries, keys, values)

    packed = dict(zip(FIRST, pack(FIRST, PACK_MB, queries, keys, values)))
    others = [r for r in range(n) if r not in FIRST]
    arrays = lax.optimization_barrier((queries, keys, values, packed[FIRST[0]]))[:3]
    packed.update(zip(others, pack(others, 6, *arrays)))
    per = n // cores
    rounds = [
        [
            (z * cores + c, (c * per + (z ^ r) // cores) * cores + (z ^ r) % cores)
            for z in range(n)
            for c in range(cores)
        ]
        for r in range(n)
    ]
    bias = pl.pallas_call(
        functools.partial(bias_kernel, n, cores, tokens),
        out_shape=jax.ShapeDtypeStruct((n * half, n * length), jnp.float32),
        in_specs=[SMEM, SMEM],
        out_specs=VMEM,
        compiler_params=pltpu.CompilerParams(vmem_limit_bytes=4 * 2**20),
        name="bias",
    )(band_table, windows)
    blocks = [packed[r] for r in range(n)]
    blocks[TIE], _ = lax.optimization_barrier((packed[TIE], bias))
    own = [lax.ppermute(blocks[r], ("tm", "sub"), rounds[r]) for r in range(n)]
    weight, _ = lax.optimization_barrier((out_weight, packed[W_AFTER]))
    other_weight = swapped(weight, "sub")
    other = []
    for r in range(n):
        other.append(swapped(own[r], "sub"))
    bias, other_weight = lax.optimization_barrier((bias, other_weight))

    travels = list(zip(*layout(n)))
    outs = pl.pallas_call(
        functools.partial(attend_kernel, n, cores, tokens),
        out_shape=[jax.ShapeDtypeStruct((len(chunks) * rows, wide), bf16) for _, chunks in travels],
        in_specs=[VMEM] * (1 + 2 * n),
        out_specs=[VMEM] * len(travels),
        scratch_shapes=[
            pltpu.VMEM((2, n * half, n * length), jnp.float32),
            pltpu.VMEM((2, n * half, n * length), bf16),
            pltpu.VMEM((n, half, wide), bf16),
        ],
        compiler_params=pltpu.CompilerParams(vmem_limit_bytes=24 * 2**20),
        name="attend",
    )(bias, *own, *other)
    back = [
        (k, chunks, lax.ppermute(out, "tm", [(z, z ^ k) for z in range(n)]) if k else out)
        for (k, chunks), out in zip(travels, outs)
    ]
    sums = []
    for a in range(CHUNKS):
        held = [(k, chunks.index(a) * rows, part) for k, chunks, part in back if a in chunks]
        places = [(k, first) for k, first, _ in held]
        parts = [part for _, _, part in held]
        keep, send = pl.pallas_call(
            functools.partial(project_kernel, n, cores, places),
            out_shape=[
                jax.ShapeDtypeStruct((count, model), jnp.float32),
                jax.ShapeDtypeStruct((count, model), bf16),
            ],
            in_specs=[VMEM] * (2 + n),
            out_specs=[VMEM] * 2,
            scratch_shapes=[pltpu.VMEM((n, rows, wide), bf16)],
            compiler_params=pltpu.CompilerParams(vmem_limit_bytes=24 * 2**20),
            name="project",
        )(out_weight, other_weight, *parts)
        sums += [keep, swapped(send, "head")]
    return pl.pallas_call(
        functools.partial(add_kernel, CHUNKS),
        out_shape=jax.ShapeDtypeStruct((1, tokens, model), bf16),
        in_specs=[VMEM] * (2 * CHUNKS),
        out_specs=VMEM,
        compiler_params=pltpu.CompilerParams(vmem_limit_bytes=4 * 2**20),
        name="add",
    )(*sums)


def solution(mesh):
    n, cores, xs = mesh.shape["tm"], mesh.shape["sub"], mesh.shape["head"]

    def local(queries, keys, values, band_table, windows, out_weight):
        frames, length, width = queries.shape
        fits = (
            frames == 1
            and n & (n - 1) == 0
            and cores == 2
            and xs == 2
            and n % cores == 0
            and width * cores % (n * HEAD) == 0
            and length % (xs * cores * CHUNKS * 16) == 0
        )
        step = functools.partial(spread, n, cores) if fits else gathered
        return step(queries, keys, values, band_table, windows, out_weight)

    return jax.shard_map(
        local,
        mesh=mesh,
        in_specs=(
            P(("clip", "tm"), None, ("head", "sub")),
            P(("clip", "tm"), None, ("head", "sub")),
            P(("clip", "tm"), None, ("head", "sub")),
            P(),
            P(),
            P(("head", "sub"), None),
        ),
        out_specs=P(("clip", "tm"), ("head", "sub"), None),
        check_vma=False,
    )
```

```python
import functools

import jax
import jax.numpy as jnp
from jax import lax
from jax.experimental import pallas as pl
from jax.experimental.pallas import tpu as pltpu
from jax.sharding import PartitionSpec as P

HEAD = 128
ANY = pl.BlockSpec(memory_space=pl.ANY)
VMEM = pl.BlockSpec(memory_space=pltpu.VMEM)
HBM = pl.BlockSpec(memory_space=pltpu.HBM)
SMEM = pl.BlockSpec(memory_space=pltpu.SMEM)
CHUNKS = 2
ACROSS = 64
PACK_MB = 59
TIE = 0
FIRST = [2]
W_AFTER = 2


def gathered(queries, keys, values, band_table, windows, out_weight):
    frames, length, width = queries.shape
    heads = width // HEAD
    scale = HEAD ** (-0.5)
    here = lax.axis_index("tm") * frames
    query = queries[0].reshape(length, heads, HEAD)
    places = lax.iota(jnp.int32, length)
    gap = jnp.abs(places[:, None] - places[None, :])

    def absorb(carry, key_frame, value_frame, frame):
        peak, total, numer = carry
        reach = windows[band_table[here, frame]]
        allowed = (gap <= reach)[None]
        scores = (
            jnp.einsum(
                "phd,qhd->hpq",
                query,
                key_frame.reshape(length, heads, HEAD),
                preferred_element_type=jnp.float32,
            )
            * scale
        )
        masked = jnp.where(allowed, scores, jnp.float32(-1e30))
        top = jnp.maximum(peak, jnp.max(masked, axis=-1))
        weights = jnp.where(allowed, jnp.exp(scores - top[:, :, None]), jnp.float32(0.0))
        shrink = jnp.exp(peak - top)
        total = total * shrink + jnp.sum(weights, axis=-1)
        added = jnp.einsum(
            "hpq,qhd->phd",
            weights.astype(jnp.bfloat16),
            value_frame.reshape(length, heads, HEAD),
            preferred_element_type=jnp.float32,
        )
        numer = numer * jnp.transpose(shrink)[:, :, None] + added
        return (top, total, numer)

    carry = (
        jnp.full((heads, length), -1e30, jnp.float32),
        jnp.zeros((heads, length), jnp.float32),
        jnp.zeros((length, heads, HEAD), jnp.float32),
    )
    key_part = lax.all_gather(keys, "tm", axis=0, tiled=True)
    value_part = lax.all_gather(values, "tm", axis=0, tiled=True)

    def advance(inner, item):
        return (absorb(inner, *item), None)

    state, _ = lax.scan(
        advance, carry, (key_part, value_part, lax.iota(jnp.int32, key_part.shape[0]))
    )
    _, total, numer = state
    attended = (
        (numer / jnp.transpose(total)[:, :, None]).astype(jnp.bfloat16).reshape(length, width)
    )
    mixed = lax.psum_scatter(
        jnp.dot(attended, out_weight, preferred_element_type=jnp.float32).astype(jnp.bfloat16),
        ("head", "sub"),
        scatter_dimension=0,
        tiled=True,
    )
    return mixed[None]


def run_copies(copies, sem):
    started = [pltpu.make_async_copy(s, d, sem.at[i]) for i, (s, d) in enumerate(copies)]
    for copy in started:
        copy.start()
    for copy in started:
        copy.wait()


def pack_kernel(n, cores, tokens, rounds, q_ref, k_ref, v_ref, *rest):
    outs, sem = rest[: len(rounds)], rest[len(rounds)]
    z = lax.axis_index("tm")
    _, half, wide = outs[0].shape
    copies = []
    for r, out in zip(rounds, outs):
        t = z ^ r
        cols = pl.ds(pl.multiple_of((t // cores) * wide, wide), wide)
        b = t % cores
        rows = pl.ds(pl.multiple_of(b * half, half), half)
        copies.append((k_ref.at[0, rows, cols], out.at[0]))
        copies.append((v_ref.at[0, rows, cols], out.at[1]))
        for i in range(half // tokens):
            place = pl.ds(pl.multiple_of(((i ^ b) * cores + b) * tokens, tokens), tokens)
            copies.append((q_ref.at[0, place, cols], out.at[2, pl.ds(i * tokens, tokens)]))
    run_copies(copies, sem)


def bias_kernel(n, cores, tokens, band_ref, reach_ref, bias_ref):
    z, c = lax.axis_index("tm"), lax.axis_index("sub")
    length = bias_ref.shape[1] // n
    half = length // cores
    t = (z % (n // cores)) * cores + c
    row = lax.broadcasted_iota(jnp.int32, (half, length), 0)
    key = lax.broadcasted_iota(jnp.int32, (half, length), 1)
    place = ((row // tokens ^ c) * cores + c) * tokens + row % tokens
    key_place = jnp.where(key < half, key + c * half, key - half + (1 - c) * half)
    gap = jnp.abs(place - key_place)
    for r in range(n):
        for s in range(n):
            reach = reach_ref[band_ref[t ^ r, t ^ s]]
            bias_ref[r * half : (r + 1) * half, s * length : (s + 1) * length] = jnp.where(
                gap <= reach, jnp.float32(0.0), jnp.float32(-1e30)
            )


RATE = HEAD ** (-0.5) * 1.4426950408889634
LAST = 1


def hidden(tokens, half, r, at, s, g):
    return tokens >= ACROSS and at == 0 and r != s and g >= half


def attend_early_kernel(n, cores, tokens, bias_ref, *rest):
    own, other = rest[:n], rest[n : 2 * n - 1]
    numer_ref, total_ref, top_ref, s_all, p_all = rest[2 * n - 1 :]
    half = own[0].shape[1]
    heads = own[0].shape[2] // HEAD
    length = half * cores
    rate = jnp.float32(RATE)
    keyed = [
        (s, g) for s in range(n) for g in range(0, length, 128) if s != LAST or g < half
    ]
    places = [(r, at) for r in range(n) for at in range(0, half, tokens)]

    def both(i, s, cols):
        mine = own[s][i, :, cols]
        if s == LAST:
            return mine
        return jnp.concatenate([mine, other[(s ^ 1) - 1][i, :, cols]])

    for slot in range(2):
        for r, at in places:
            for s, g in keyed:
                if hidden(tokens, half, r, at, s, g):
                    lines = slice(r * half + at, r * half + at + tokens)
                    p_all[slot, lines, s * length + g : s * length + g + 128] = jnp.zeros(
                        (tokens, 128), jnp.bfloat16
                    )

    def score(h, s):
        cols = slice(h * HEAD, (h + 1) * HEAD)
        q = jnp.concatenate([own[r][2, :, cols] for r in range(n)])
        k = both(0, s, cols)
        s_all[h % 2, :, s * length : s * length + k.shape[0]] = lax.dot_general(
            q, k, (((1,), (1,)), ((), ())), preferred_element_type=jnp.float32
        )

    def soften(h, r, at):
        used = [s * length + g for s, g in keyed if not hidden(tokens, half, r, at, s, g)]
        for step in range(r * half + at, r * half + at + tokens, 16):
            lines = slice(step, step + 16)
            parts = [
                s_all[h % 2, lines, g : g + 128] + bias_ref[lines, g : g + 128] for g in used
            ]
            top = jnp.max(functools.reduce(jnp.maximum, parts), axis=1, keepdims=True)
            top_ref[h, lines, :] = jnp.broadcast_to(top, (16, HEAD))
            for g, part in zip(used, parts):
                p_all[h % 2, lines, g : g + 128] = jnp.exp2((part - top) * rate).astype(
                    jnp.bfloat16
                )

    def mix(h, r):
        cols = slice(h * HEAD, (h + 1) * HEAD)
        numer = 0.0
        lines = slice(r * half, (r + 1) * half)
        for s in range(n):
            v = both(1, s, cols)
            numer += jnp.dot(
                p_all[h % 2, lines, s * length : s * length + v.shape[0]],
                jnp.concatenate([v, jnp.ones_like(v)], axis=1),
                preferred_element_type=jnp.float32,
            )
        numer_ref[h, lines, :] = numer[:, :HEAD]
        total_ref[h, lines, :] = numer[:, HEAD:]

    for s in range(n):
        score(0, s)
    for h in range(heads):
        for r in range(n):
            if h + 1 < heads:
                score(h + 1, r)
            for at in range(0, half, tokens):
                soften(h, r, at)
            mix(h, r)


def attend_late_kernel(n, cores, tokens, start, count, bias_ref, numer_ref, total_ref, top_ref, *rest):
    own, other, outs = rest[:n], rest[n], rest[n + 1 : -4]
    s_all, p_all, f_all, o_all = rest[-4:]
    z, c = lax.axis_index("tm"), lax.axis_index("sub")
    half = own[0].shape[1]
    heads = own[0].shape[2] // HEAD
    length = half * cores
    t = (z % (n // cores)) * cores + c
    rate = jnp.float32(RATE)
    first = LAST * length + half
    seen = [
        (r, at)
        for r in range(n)
        for at in range(0, half, tokens)
        if not hidden(tokens, half, r, at, LAST, half)
    ]

    def score(h):
        cols = slice(h * HEAD, (h + 1) * HEAD)
        q = jnp.concatenate([own[r][2, at + start : at + start + count, cols] for r, at in seen])
        s_all[h] = lax.dot_general(
            q, other[0, :, cols], (((1,), (1,)), ((), ())), preferred_element_type=jnp.float32
        )

    for h in range(heads):
        score(h)
    for h in range(heads):
        cols = slice(h * HEAD, (h + 1) * HEAD)
        for i, (r, at) in enumerate(seen):
            for step in range(0, count, 16):
                lines = slice(i * count + step, i * count + step + 16)
                base = r * half + at + start + step
                place = slice(base, base + 16)
                parts = [
                    s_all[h, lines, g : g + 128] + bias_ref[place, first + g : first + g + 128]
                    for g in range(0, half, 128)
                ]
                old = top_ref[h, place, :]
                top = jnp.max(functools.reduce(jnp.maximum, parts), axis=1, keepdims=True)
                top = jnp.maximum(old, top)
                f_all[h, lines, :] = jnp.exp2((old - top) * rate)
                for g, part in zip(range(0, half, 128), parts):
                    p_all[h, lines, g : g + 128] = jnp.exp2((part - top[:, :1]) * rate).astype(
                        jnp.bfloat16
                    )
        v = other[1, :, cols]
        added = jnp.dot(
            p_all[h], jnp.concatenate([v, jnp.ones_like(v)], axis=1),
            preferred_element_type=jnp.float32,
        )
        for r in range(n):
            for b, at in enumerate(range(0, half, tokens)):
                place = slice(r * half + at + start, r * half + at + start + count)
                numer, total = numer_ref[h, place, :], total_ref[h, place, :]
                if (r, at) in seen:
                    i = seen.index((r, at)) * count
                    shrink = f_all[h, i : i + count, :]
                    numer = numer * shrink + added[i : i + count, :HEAD]
                    total = total * shrink + added[i : i + count, HEAD:]
                o_all[r, b * count : (b + 1) * count, cols] = (numer / total).astype(jnp.bfloat16)

    for i, out in enumerate(outs):
        out[...] = o_all[t ^ z ^ (n - 1 - i)]


def project_kernel(n, cores, places, own_w, other_w, *rest):
    parts = rest[:n]
    keep_ref, send_ref, a_all = rest[n:]
    z, c, x = lax.axis_index("tm"), lax.axis_index("sub"), lax.axis_index("head")
    count = keep_ref.shape[0]
    for (k, first), part in zip(places, parts):
        for b in range(2):
            at = pl.ds(pl.multiple_of((b ^ 1 ^ x ^ c) * count + first, count), count)
            a_all[z ^ k, b * count : (b + 1) * count] = part[at, :]
    per = n // cores
    wide = a_all.shape[2]
    total = 0.0
    for w_ref, core in ((own_w, c), (other_w, 1 - c)):
        for g in range(per):
            total += jnp.dot(
                a_all[core * per + g], w_ref[g * wide : (g + 1) * wide, :],
                preferred_element_type=jnp.float32,
            )
    send_ref[...] = total[:count].astype(send_ref.dtype)
    keep_ref[...] = total[count:]


def add_kernel(chunks, *refs):
    out_ref = refs[-1]
    for a in range(chunks):
        keep, got = refs[2 * a], refs[2 * a + 1]
        count = keep.shape[0]
        out_ref[0, a * count : (a + 1) * count] = (
            keep[...] + got[...].astype(jnp.float32)
        ).astype(out_ref.dtype)


def swapped(x, axis):
    return lax.ppermute(x, axis, [(0, 1), (1, 0)])


def spread(n, cores, queries, keys, values, band_table, windows, out_weight):
    _, length, width = queries.shape
    depth, model = out_weight.shape
    wide = width * cores // n
    half = length // cores
    tokens = half // 2
    count = tokens // CHUNKS
    rows = 2 * count
    bf16 = queries.dtype

    def pack(rounds, mb, queries, keys, values):
        return pl.pallas_call(
            functools.partial(pack_kernel, n, cores, tokens, rounds),
            out_shape=[jax.ShapeDtypeStruct((3, half, wide), bf16)] * len(rounds),
            in_specs=[ANY] * 3,
            out_specs=[VMEM] * len(rounds),
            scratch_shapes=[pltpu.SemaphoreType.DMA((4 * len(rounds),))],
            compiler_params=pltpu.CompilerParams(vmem_limit_bytes=mb * 2**20),
            name="pack",
        )(queries, keys, values)

    packed = dict(zip(FIRST, pack(FIRST, PACK_MB, queries, keys, values)))
    others = [r for r in range(n) if r not in FIRST]
    arrays = lax.optimization_barrier((queries, keys, values, packed[FIRST[0]]))[:3]
    packed.update(zip(others, pack(others, 6, *arrays)))
    per = n // cores
    rounds = [
        [
            (z * cores + c, (c * per + (z ^ r) // cores) * cores + (z ^ r) % cores)
            for z in range(n)
            for c in range(cores)
        ]
        for r in range(n)
    ]
    bias = pl.pallas_call(
        functools.partial(bias_kernel, n, cores, tokens),
        out_shape=jax.ShapeDtypeStruct((n * half, n * length), jnp.float32),
        in_specs=[SMEM, SMEM],
        out_specs=VMEM,
        compiler_params=pltpu.CompilerParams(vmem_limit_bytes=4 * 2**20),
        name="bias",
    )(band_table, windows)
    blocks = [packed[r] for r in range(n)]
    blocks[TIE], _ = lax.optimization_barrier((packed[TIE], bias))
    own = [lax.ppermute(blocks[r], ("tm", "sub"), rounds[r]) for r in range(n)]
    weight, _ = lax.optimization_barrier((out_weight, packed[W_AFTER]))
    other_weight = swapped(weight, "sub")
    other = []
    for r in range(n):
        other.append(swapped(own[r], "sub"))
    bias, other_weight = lax.optimization_barrier((bias, other_weight))

    heads = wide // HEAD
    f32 = jnp.float32
    partial = pl.pallas_call(
        functools.partial(attend_early_kernel, n, cores, tokens),
        out_shape=[jax.ShapeDtypeStruct((heads, n * half, HEAD), f32)] * 3,
        in_specs=[VMEM] * (2 * n),
        out_specs=[VMEM] * 3,
        scratch_shapes=[
            pltpu.VMEM((2, n * half, n * length), f32),
            pltpu.VMEM((2, n * half, n * length), bf16),
        ],
        compiler_params=pltpu.CompilerParams(vmem_limit_bytes=24 * 2**20),
        name="attend_early",
    )(bias, *own, *other[1:])
    blocks_seen = 2 * n if tokens < ACROSS else n + 1
    back = []
    for a in range(CHUNKS):
        outs = pl.pallas_call(
            functools.partial(attend_late_kernel, n, cores, tokens, a * count, count),
            out_shape=[jax.ShapeDtypeStruct((rows, wide), bf16)] * n,
            in_specs=[VMEM] * (5 + n),
            out_specs=[VMEM] * n,
            scratch_shapes=[
                pltpu.VMEM((heads, blocks_seen * count, half), f32),
                pltpu.VMEM((heads, blocks_seen * count, half), bf16),
                pltpu.VMEM((heads, blocks_seen * count, HEAD), f32),
                pltpu.VMEM((n, rows, wide), bf16),
            ],
            compiler_params=pltpu.CompilerParams(vmem_limit_bytes=24 * 2**20),
            name="attend_late",
        )(bias, *partial, *own, other[0])
        for i, out in enumerate(outs):
            k = n - 1 - i
            pairs = [(z, z ^ k) for z in range(n)]
            back.append((k, [a], lax.ppermute(out, "tm", pairs) if k else out))
    sums = []
    for a in range(CHUNKS):
        held = [(k, chunks.index(a) * rows, part) for k, chunks, part in back if a in chunks]
        places = [(k, first) for k, first, _ in held]
        parts = [part for _, _, part in held]
        keep, send = pl.pallas_call(
            functools.partial(project_kernel, n, cores, places),
            out_shape=[
                jax.ShapeDtypeStruct((count, model), jnp.float32),
                jax.ShapeDtypeStruct((count, model), bf16),
            ],
            in_specs=[VMEM] * (2 + n),
            out_specs=[VMEM] * 2,
            scratch_shapes=[pltpu.VMEM((n, rows, wide), bf16)],
            compiler_params=pltpu.CompilerParams(vmem_limit_bytes=24 * 2**20),
            name="project",
        )(out_weight, other_weight, *parts)
        sums += [keep, swapped(send, "head")]
    return pl.pallas_call(
        functools.partial(add_kernel, CHUNKS),
        out_shape=jax.ShapeDtypeStruct((1, tokens, model), bf16),
        in_specs=[VMEM] * (2 * CHUNKS),
        out_specs=VMEM,
        compiler_params=pltpu.CompilerParams(vmem_limit_bytes=4 * 2**20),
        name="add",
    )(*sums)


def solution(mesh):
    n, cores, xs = mesh.shape["tm"], mesh.shape["sub"], mesh.shape["head"]

    def local(queries, keys, values, band_table, windows, out_weight):
        frames, length, width = queries.shape
        fits = (
            frames == 1
            and n > 2
            and n & (n - 1) == 0
            and cores == 2
            and xs == 2
            and n % cores == 0
            and width * cores % (n * HEAD) == 0
            and length % (xs * cores * CHUNKS * 16) == 0
        )
        step = functools.partial(spread, n, cores) if fits else gathered
        return step(queries, keys, values, band_table, windows, out_weight)

    return jax.shard_map(
        local,
        mesh=mesh,
        in_specs=(
            P(("clip", "tm"), None, ("head", "sub")),
            P(("clip", "tm"), None, ("head", "sub")),
            P(("clip", "tm"), None, ("head", "sub")),
            P(),
            P(),
            P(("head", "sub"), None),
        ),
        out_specs=P(("clip", "tm"), ("head", "sub"), None),
        check_vma=False,
    )
```

```python
import functools

import jax
import jax.numpy as jnp
from jax import lax
from jax.experimental import pallas as pl
from jax.experimental.pallas import tpu as pltpu
from jax.sharding import PartitionSpec as P

HEAD = 128
ANY = pl.BlockSpec(memory_space=pl.ANY)
VMEM = pl.BlockSpec(memory_space=pltpu.VMEM)
HBM = pl.BlockSpec(memory_space=pltpu.HBM)
SMEM = pl.BlockSpec(memory_space=pltpu.SMEM)
CHUNKS = 2
ACROSS = 64
PACK_MB = 59
TIE = 0
FIRST = [2]
W_AFTER = 2


def gathered(queries, keys, values, band_table, windows, out_weight):
    frames, length, width = queries.shape
    heads = width // HEAD
    scale = HEAD ** (-0.5)
    here = lax.axis_index("tm") * frames
    query = queries[0].reshape(length, heads, HEAD)
    places = lax.iota(jnp.int32, length)
    gap = jnp.abs(places[:, None] - places[None, :])

    def absorb(carry, key_frame, value_frame, frame):
        peak, total, numer = carry
        reach = windows[band_table[here, frame]]
        allowed = (gap <= reach)[None]
        scores = (
            jnp.einsum(
                "phd,qhd->hpq",
                query,
                key_frame.reshape(length, heads, HEAD),
                preferred_element_type=jnp.float32,
            )
            * scale
        )
        masked = jnp.where(allowed, scores, jnp.float32(-1e30))
        top = jnp.maximum(peak, jnp.max(masked, axis=-1))
        weights = jnp.where(allowed, jnp.exp(scores - top[:, :, None]), jnp.float32(0.0))
        shrink = jnp.exp(peak - top)
        total = total * shrink + jnp.sum(weights, axis=-1)
        added = jnp.einsum(
            "hpq,qhd->phd",
            weights.astype(jnp.bfloat16),
            value_frame.reshape(length, heads, HEAD),
            preferred_element_type=jnp.float32,
        )
        numer = numer * jnp.transpose(shrink)[:, :, None] + added
        return (top, total, numer)

    carry = (
        jnp.full((heads, length), -1e30, jnp.float32),
        jnp.zeros((heads, length), jnp.float32),
        jnp.zeros((length, heads, HEAD), jnp.float32),
    )
    key_part = lax.all_gather(keys, "tm", axis=0, tiled=True)
    value_part = lax.all_gather(values, "tm", axis=0, tiled=True)

    def advance(inner, item):
        return (absorb(inner, *item), None)

    state, _ = lax.scan(
        advance, carry, (key_part, value_part, lax.iota(jnp.int32, key_part.shape[0]))
    )
    _, total, numer = state
    attended = (
        (numer / jnp.transpose(total)[:, :, None]).astype(jnp.bfloat16).reshape(length, width)
    )
    mixed = lax.psum_scatter(
        jnp.dot(attended, out_weight, preferred_element_type=jnp.float32).astype(jnp.bfloat16),
        ("head", "sub"),
        scatter_dimension=0,
        tiled=True,
    )
    return mixed[None]


def run_copies(copies, sem):
    started = [pltpu.make_async_copy(s, d, sem.at[i]) for i, (s, d) in enumerate(copies)]
    for copy in started:
        copy.start()
    for copy in started:
        copy.wait()


def pack_kernel(n, cores, tokens, rounds, q_ref, k_ref, v_ref, *rest):
    outs, sem = rest[: len(rounds)], rest[len(rounds)]
    z = lax.axis_index("tm")
    _, half, wide = outs[0].shape
    copies = []
    for r, out in zip(rounds, outs):
        t = z ^ r
        cols = pl.ds(pl.multiple_of((t // cores) * wide, wide), wide)
        b = t % cores
        rows = pl.ds(pl.multiple_of(b * half, half), half)
        copies.append((k_ref.at[0, rows, cols], out.at[0]))
        copies.append((v_ref.at[0, rows, cols], out.at[1]))
        for i in range(half // tokens):
            place = pl.ds(pl.multiple_of(((i ^ b) * cores + b) * tokens, tokens), tokens)
            copies.append((q_ref.at[0, place, cols], out.at[2, pl.ds(i * tokens, tokens)]))
    run_copies(copies, sem)


def bias_kernel(n, cores, tokens, band_ref, reach_ref, bias_ref):
    z, c = lax.axis_index("tm"), lax.axis_index("sub")
    length = bias_ref.shape[1] // n
    half = length // cores
    t = (z % (n // cores)) * cores + c
    row = lax.broadcasted_iota(jnp.int32, (half, length), 0)
    key = lax.broadcasted_iota(jnp.int32, (half, length), 1)
    place = ((row // tokens ^ c) * cores + c) * tokens + row % tokens
    key_place = jnp.where(key < half, key + c * half, key - half + (1 - c) * half)
    gap = jnp.abs(place - key_place)
    for r in range(n):
        for s in range(n):
            reach = reach_ref[band_ref[t ^ r, t ^ s]]
            bias_ref[r * half : (r + 1) * half, s * length : (s + 1) * length] = jnp.where(
                gap <= reach, jnp.float32(0.0), jnp.float32(-1e30)
            )


RATE = HEAD ** (-0.5) * 1.4426950408889634
LAST = 1


def hidden(tokens, half, r, at, s, g):
    return tokens >= ACROSS and at == 0 and r != s and g >= half


def attend_early_kernel(n, cores, tokens, bias_ref, *rest):
    own, other = rest[:n], rest[n : 2 * n - 1]
    numer_ref, total_ref, top_ref, s_all, p_all = rest[2 * n - 1 :]
    half = own[0].shape[1]
    heads = own[0].shape[2] // HEAD
    length = half * cores
    rate = jnp.float32(RATE)
    keyed = [
        (s, g) for s in range(n) for g in range(0, length, 128) if s != LAST or g < half
    ]
    places = [(r, at) for r in range(n) for at in range(0, half, tokens)]

    def both(i, s, cols):
        mine = own[s][i, :, cols]
        if s == LAST:
            return mine
        return jnp.concatenate([mine, other[(s ^ 1) - 1][i, :, cols]])

    for slot in range(2):
        for r, at in places:
            for s, g in keyed:
                if hidden(tokens, half, r, at, s, g):
                    lines = slice(r * half + at, r * half + at + tokens)
                    p_all[slot, lines, s * length + g : s * length + g + 128] = jnp.zeros(
                        (tokens, 128), jnp.bfloat16
                    )

    def score(h, s):
        cols = slice(h * HEAD, (h + 1) * HEAD)
        q = jnp.concatenate([own[r][2, :, cols] for r in range(n)])
        k = both(0, s, cols)
        s_all[h % 2, :, s * length : s * length + k.shape[0]] = lax.dot_general(
            q, k, (((1,), (1,)), ((), ())), preferred_element_type=jnp.float32
        )

    def soften(h, r, at):
        used = [s * length + g for s, g in keyed if not hidden(tokens, half, r, at, s, g)]
        for step in range(r * half + at, r * half + at + tokens, 16):
            lines = slice(step, step + 16)
            parts = [
                s_all[h % 2, lines, g : g + 128] + bias_ref[lines, g : g + 128] for g in used
            ]
            top = jnp.max(functools.reduce(jnp.maximum, parts), axis=1, keepdims=True)
            top_ref[h, lines, :] = jnp.broadcast_to(top, (16, HEAD))
            for g, part in zip(used, parts):
                p_all[h % 2, lines, g : g + 128] = jnp.exp2((part - top) * rate).astype(
                    jnp.bfloat16
                )

    def mix(h, r):
        cols = slice(h * HEAD, (h + 1) * HEAD)
        numer = 0.0
        lines = slice(r * half, (r + 1) * half)
        for s in range(n):
            v = both(1, s, cols)
            numer += jnp.dot(
                p_all[h % 2, lines, s * length : s * length + v.shape[0]],
                jnp.concatenate([v, jnp.ones_like(v)], axis=1),
                preferred_element_type=jnp.float32,
            )
        numer_ref[h, lines, :] = numer[:, :HEAD]
        total_ref[h, lines, :] = numer[:, HEAD:]

    for s in range(n):
        score(0, s)
    for h in range(heads):
        for r in range(n):
            if h + 1 < heads:
                score(h + 1, r)
            for at in range(0, half, tokens):
                soften(h, r, at)
            mix(h, r)


def attend_late_kernel(n, cores, tokens, start, count, bias_ref, numer_ref, total_ref, top_ref, *rest):
    own, other, outs = rest[:n], rest[n], rest[n + 1 : -4]
    s_all, p_all, f_all, o_all = rest[-4:]
    z, c = lax.axis_index("tm"), lax.axis_index("sub")
    half = own[0].shape[1]
    heads = own[0].shape[2] // HEAD
    length = half * cores
    t = (z % (n // cores)) * cores + c
    rate = jnp.float32(RATE)
    first = LAST * length + half
    seen = [
        (r, at)
        for r in range(n)
        for at in range(0, half, tokens)
        if not hidden(tokens, half, r, at, LAST, half)
    ]

    def score(h):
        cols = slice(h * HEAD, (h + 1) * HEAD)
        q = jnp.concatenate([own[r][2, at + start : at + start + count, cols] for r, at in seen])
        s_all[h] = lax.dot_general(
            q, other[0, :, cols], (((1,), (1,)), ((), ())), preferred_element_type=jnp.float32
        )

    for h in range(heads):
        score(h)
    for h in range(heads):
        cols = slice(h * HEAD, (h + 1) * HEAD)
        for i, (r, at) in enumerate(seen):
            for step in range(0, count, 16):
                lines = slice(i * count + step, i * count + step + 16)
                base = r * half + at + start + step
                place = slice(base, base + 16)
                parts = [
                    s_all[h, lines, g : g + 128] + bias_ref[place, first + g : first + g + 128]
                    for g in range(0, half, 128)
                ]
                old = top_ref[h, place, :]
                top = jnp.max(functools.reduce(jnp.maximum, parts), axis=1, keepdims=True)
                top = jnp.maximum(old, top)
                f_all[h, lines, :] = jnp.exp2((old - top) * rate)
                for g, part in zip(range(0, half, 128), parts):
                    p_all[h, lines, g : g + 128] = jnp.exp2((part - top[:, :1]) * rate).astype(
                        jnp.bfloat16
                    )
        v = other[1, :, cols]
        added = jnp.dot(
            p_all[h], jnp.concatenate([v, jnp.ones_like(v)], axis=1),
            preferred_element_type=jnp.float32,
        )
        for r in range(n):
            for b, at in enumerate(range(0, half, tokens)):
                place = slice(r * half + at + start, r * half + at + start + count)
                numer, total = numer_ref[h, place, :], total_ref[h, place, :]
                if (r, at) in seen:
                    i = seen.index((r, at)) * count
                    shrink = f_all[h, i : i + count, :]
                    numer = numer * shrink + added[i : i + count, :HEAD]
                    total = total * shrink + added[i : i + count, HEAD:]
                o_all[r, b * count : (b + 1) * count, cols] = (numer / total).astype(jnp.bfloat16)

    for i, out in enumerate(outs):
        out[...] = o_all[t ^ z ^ (n - 1 - i)]


def project_kernel(n, cores, places, own_w, other_w, *rest):
    parts = rest[:n]
    keep_ref, send_ref, a_all = rest[n:]
    z, c, x = lax.axis_index("tm"), lax.axis_index("sub"), lax.axis_index("head")
    count = keep_ref.shape[0]
    for (k, first), part in zip(places, parts):
        for b in range(2):
            at = pl.ds(pl.multiple_of((b ^ 1 ^ x ^ c) * count + first, count), count)
            a_all[z ^ k, b * count : (b + 1) * count] = part[at, :]
    per = n // cores
    wide = a_all.shape[2]
    total = 0.0
    for w_ref, core in ((own_w, c), (other_w, 1 - c)):
        for g in range(per):
            total += jnp.dot(
                a_all[core * per + g], w_ref[g * wide : (g + 1) * wide, :],
                preferred_element_type=jnp.float32,
            )
    send_ref[...] = total[:count].astype(send_ref.dtype)
    keep_ref[...] = total[count:]


def add_kernel(first, keep_ref, got_ref, *rest):
    out_ref, sum_ref, sem = rest[-3:]
    count = keep_ref.shape[0]
    sum_ref[...] = (keep_ref[...] + got_ref[...].astype(jnp.float32)).astype(sum_ref.dtype)
    run_copies([(sum_ref, out_ref.at[0, pl.ds(first, count)])], sem)


def swapped(x, axis):
    return lax.ppermute(x, axis, [(0, 1), (1, 0)])


def spread(n, cores, queries, keys, values, band_table, windows, out_weight):
    _, length, width = queries.shape
    depth, model = out_weight.shape
    wide = width * cores // n
    half = length // cores
    tokens = half // 2
    count = tokens // CHUNKS
    rows = 2 * count
    bf16 = queries.dtype

    def pack(rounds, mb, queries, keys, values):
        return pl.pallas_call(
            functools.partial(pack_kernel, n, cores, tokens, rounds),
            out_shape=[jax.ShapeDtypeStruct((3, half, wide), bf16)] * len(rounds),
            in_specs=[ANY] * 3,
            out_specs=[VMEM] * len(rounds),
            scratch_shapes=[pltpu.SemaphoreType.DMA((4 * len(rounds),))],
            compiler_params=pltpu.CompilerParams(vmem_limit_bytes=mb * 2**20),
            name="pack",
        )(queries, keys, values)

    packed = dict(zip(FIRST, pack(FIRST, PACK_MB, queries, keys, values)))
    others = [r for r in range(n) if r not in FIRST]
    arrays = lax.optimization_barrier((queries, keys, values, packed[FIRST[0]]))[:3]
    packed.update(zip(others, pack(others, 6, *arrays)))
    per = n // cores
    rounds = [
        [
            (z * cores + c, (c * per + (z ^ r) // cores) * cores + (z ^ r) % cores)
            for z in range(n)
            for c in range(cores)
        ]
        for r in range(n)
    ]
    bias = pl.pallas_call(
        functools.partial(bias_kernel, n, cores, tokens),
        out_shape=jax.ShapeDtypeStruct((n * half, n * length), jnp.float32),
        in_specs=[SMEM, SMEM],
        out_specs=VMEM,
        compiler_params=pltpu.CompilerParams(vmem_limit_bytes=4 * 2**20),
        name="bias",
    )(band_table, windows)
    blocks = [packed[r] for r in range(n)]
    blocks[TIE], _ = lax.optimization_barrier((packed[TIE], bias))
    own = [lax.ppermute(blocks[r], ("tm", "sub"), rounds[r]) for r in range(n)]
    weight, _ = lax.optimization_barrier((out_weight, packed[W_AFTER]))
    other_weight = swapped(weight, "sub")
    other = []
    for r in range(n):
        other.append(swapped(own[r], "sub"))
    bias, other_weight = lax.optimization_barrier((bias, other_weight))

    heads = wide // HEAD
    f32 = jnp.float32
    partial = pl.pallas_call(
        functools.partial(attend_early_kernel, n, cores, tokens),
        out_shape=[jax.ShapeDtypeStruct((heads, n * half, HEAD), f32)] * 3,
        in_specs=[VMEM] * (2 * n),
        out_specs=[VMEM] * 3,
        scratch_shapes=[
            pltpu.VMEM((2, n * half, n * length), f32),
            pltpu.VMEM((2, n * half, n * length), bf16),
        ],
        compiler_params=pltpu.CompilerParams(vmem_limit_bytes=24 * 2**20),
        name="attend_early",
    )(bias, *own, *other[1:])
    blocks_seen = 2 * n if tokens < ACROSS else n + 1
    back = []
    for a in range(CHUNKS):
        outs = pl.pallas_call(
            functools.partial(attend_late_kernel, n, cores, tokens, a * count, count),
            out_shape=[jax.ShapeDtypeStruct((rows, wide), bf16)] * n,
            in_specs=[VMEM] * (5 + n),
            out_specs=[VMEM] * n,
            scratch_shapes=[
                pltpu.VMEM((heads, blocks_seen * count, half), f32),
                pltpu.VMEM((heads, blocks_seen * count, half), bf16),
                pltpu.VMEM((heads, blocks_seen * count, HEAD), f32),
                pltpu.VMEM((n, rows, wide), bf16),
            ],
            compiler_params=pltpu.CompilerParams(vmem_limit_bytes=24 * 2**20),
            name="attend_late",
        )(bias, *partial, *own, other[0])
        for i, out in enumerate(outs):
            k = n - 1 - i
            pairs = [(z, z ^ k) for z in range(n)]
            back.append((k, [a], lax.ppermute(out, "tm", pairs) if k else out))
    sums = []
    for a in range(CHUNKS):
        held = [(k, chunks.index(a) * rows, part) for k, chunks, part in back if a in chunks]
        places = [(k, first) for k, first, _ in held]
        parts = [part for _, _, part in held]
        keep, send = pl.pallas_call(
            functools.partial(project_kernel, n, cores, places),
            out_shape=[
                jax.ShapeDtypeStruct((count, model), jnp.float32),
                jax.ShapeDtypeStruct((count, model), bf16),
            ],
            in_specs=[VMEM] * (2 + n),
            out_specs=[VMEM] * 2,
            scratch_shapes=[pltpu.VMEM((n, rows, wide), bf16)],
            compiler_params=pltpu.CompilerParams(vmem_limit_bytes=24 * 2**20),
            name="project",
        )(out_weight, other_weight, *parts)
        sums += [keep, swapped(send, "head")]
    mixed = []
    for a in range(CHUNKS):
        mixed = [
            pl.pallas_call(
                functools.partial(add_kernel, a * count),
                out_shape=jax.ShapeDtypeStruct((1, tokens, model), bf16),
                in_specs=[VMEM] * 2 + [ANY] * len(mixed),
                out_specs=ANY,
                scratch_shapes=[
                    pltpu.VMEM((count, model), bf16),
                    pltpu.SemaphoreType.DMA((1,)),
                ],
                input_output_aliases={2: 0} if mixed else {},
                compiler_params=pltpu.CompilerParams(vmem_limit_bytes=4 * 2**20),
                name="add",
            )(*sums[2 * a : 2 * a + 2], *mixed)
        ]
    return mixed[0]


def solution(mesh):
    n, cores, xs = mesh.shape["tm"], mesh.shape["sub"], mesh.shape["head"]

    def local(queries, keys, values, band_table, windows, out_weight):
        frames, length, width = queries.shape
        fits = (
            frames == 1
            and n > 2
            and n & (n - 1) == 0
            and cores == 2
            and xs == 2
            and n % cores == 0
            and width * cores % (n * HEAD) == 0
            and length % (xs * cores * CHUNKS * 16) == 0
        )
        step = functools.partial(spread, n, cores) if fits else gathered
        return step(queries, keys, values, band_table, windows, out_weight)

    return jax.shard_map(
        local,
        mesh=mesh,
        in_specs=(
            P(("clip", "tm"), None, ("head", "sub")),
            P(("clip", "tm"), None, ("head", "sub")),
            P(("clip", "tm"), None, ("head", "sub")),
            P(),
            P(),
            P(("head", "sub"), None),
        ),
        out_specs=P(("clip", "tm"), ("head", "sub"), None),
        check_vma=False,
    )
```

```python
import functools

import jax
import jax.numpy as jnp
from jax import lax
from jax.experimental import pallas as pl
from jax.experimental.pallas import tpu as pltpu
from jax.sharding import PartitionSpec as P

HEAD = 128
ANY = pl.BlockSpec(memory_space=pl.ANY)
VMEM = pl.BlockSpec(memory_space=pltpu.VMEM)
HBM = pl.BlockSpec(memory_space=pltpu.HBM)
SMEM = pl.BlockSpec(memory_space=pltpu.SMEM)
CHUNKS = 2
ACROSS = 64
PACK_MB = 59
TIE = 0
FIRST = [2]
W_AFTER = 2


def gathered(queries, keys, values, band_table, windows, out_weight):
    frames, length, width = queries.shape
    heads = width // HEAD
    scale = HEAD ** (-0.5)
    here = lax.axis_index("tm") * frames
    query = queries[0].reshape(length, heads, HEAD)
    places = lax.iota(jnp.int32, length)
    gap = jnp.abs(places[:, None] - places[None, :])

    def absorb(carry, key_frame, value_frame, frame):
        peak, total, numer = carry
        reach = windows[band_table[here, frame]]
        allowed = (gap <= reach)[None]
        scores = (
            jnp.einsum(
                "phd,qhd->hpq",
                query,
                key_frame.reshape(length, heads, HEAD),
                preferred_element_type=jnp.float32,
            )
            * scale
        )
        masked = jnp.where(allowed, scores, jnp.float32(-1e30))
        top = jnp.maximum(peak, jnp.max(masked, axis=-1))
        weights = jnp.where(allowed, jnp.exp(scores - top[:, :, None]), jnp.float32(0.0))
        shrink = jnp.exp(peak - top)
        total = total * shrink + jnp.sum(weights, axis=-1)
        added = jnp.einsum(
            "hpq,qhd->phd",
            weights.astype(jnp.bfloat16),
            value_frame.reshape(length, heads, HEAD),
            preferred_element_type=jnp.float32,
        )
        numer = numer * jnp.transpose(shrink)[:, :, None] + added
        return (top, total, numer)

    carry = (
        jnp.full((heads, length), -1e30, jnp.float32),
        jnp.zeros((heads, length), jnp.float32),
        jnp.zeros((length, heads, HEAD), jnp.float32),
    )
    key_part = lax.all_gather(keys, "tm", axis=0, tiled=True)
    value_part = lax.all_gather(values, "tm", axis=0, tiled=True)

    def advance(inner, item):
        return (absorb(inner, *item), None)

    state, _ = lax.scan(
        advance, carry, (key_part, value_part, lax.iota(jnp.int32, key_part.shape[0]))
    )
    _, total, numer = state
    attended = (
        (numer / jnp.transpose(total)[:, :, None]).astype(jnp.bfloat16).reshape(length, width)
    )
    mixed = lax.psum_scatter(
        jnp.dot(attended, out_weight, preferred_element_type=jnp.float32).astype(jnp.bfloat16),
        ("head", "sub"),
        scatter_dimension=0,
        tiled=True,
    )
    return mixed[None]


def run_copies(copies, sem):
    started = [pltpu.make_async_copy(s, d, sem.at[i]) for i, (s, d) in enumerate(copies)]
    for copy in started:
        copy.start()
    for copy in started:
        copy.wait()


def pack_kernel(n, cores, tokens, rounds, q_ref, k_ref, v_ref, *rest):
    outs, sem = rest[: len(rounds)], rest[len(rounds)]
    z = lax.axis_index("tm")
    _, half, wide = outs[0].shape
    copies = []
    for r, out in zip(rounds, outs):
        t = z ^ r
        cols = pl.ds(pl.multiple_of((t // cores) * wide, wide), wide)
        b = t % cores
        rows = pl.ds(pl.multiple_of(b * half, half), half)
        copies.append((k_ref.at[0, rows, cols], out.at[0]))
        copies.append((v_ref.at[0, rows, cols], out.at[1]))
        for i in range(half // tokens):
            place = pl.ds(pl.multiple_of(((i ^ b) * cores + b) * tokens, tokens), tokens)
            copies.append((q_ref.at[0, place, cols], out.at[2, pl.ds(i * tokens, tokens)]))
    run_copies(copies, sem)


def bias_kernel(n, cores, tokens, band_ref, reach_ref, bias_ref):
    z, c = lax.axis_index("tm"), lax.axis_index("sub")
    length = bias_ref.shape[1] // n
    half = length // cores
    t = (z % (n // cores)) * cores + c
    row = lax.broadcasted_iota(jnp.int32, (half, length), 0)
    key = lax.broadcasted_iota(jnp.int32, (half, length), 1)
    place = ((row // tokens ^ c) * cores + c) * tokens + row % tokens
    key_place = jnp.where(key < half, key + c * half, key - half + (1 - c) * half)
    gap = jnp.abs(place - key_place)
    for r in range(n):
        for s in range(n):
            reach = reach_ref[band_ref[t ^ r, t ^ s]]
            bias_ref[r * half : (r + 1) * half, s * length : (s + 1) * length] = jnp.where(
                gap <= reach, jnp.float32(0.0), jnp.float32(-1e30)
            )


RATE = HEAD ** (-0.5) * 1.4426950408889634
LAST = 1


def hidden(tokens, half, r, at, s, g):
    return tokens >= ACROSS and at == 0 and r != s and g >= half


def attend_early_kernel(n, cores, tokens, bias_ref, *rest):
    own, other = rest[:n], rest[n : 2 * n - 1]
    numer_ref, total_ref, top_ref, s_all, p_all = rest[2 * n - 1 :]
    half = own[0].shape[1]
    heads = own[0].shape[2] // HEAD
    length = half * cores
    rate = jnp.float32(RATE)
    keyed = [
        (s, g) for s in range(n) for g in range(0, length, 128) if s != LAST or g < half
    ]
    places = [(r, at) for r in range(n) for at in range(0, half, tokens)]

    def both(i, s, cols):
        mine = own[s][i, :, cols]
        if s == LAST:
            return mine
        return jnp.concatenate([mine, other[(s ^ 1) - 1][i, :, cols]])

    for slot in range(2):
        for r, at in places:
            for s, g in keyed:
                if hidden(tokens, half, r, at, s, g):
                    lines = slice(r * half + at, r * half + at + tokens)
                    p_all[slot, lines, s * length + g : s * length + g + 128] = jnp.zeros(
                        (tokens, 128), jnp.bfloat16
                    )

    def score(h, s):
        cols = slice(h * HEAD, (h + 1) * HEAD)
        q = jnp.concatenate([own[r][2, :, cols] for r in range(n)])
        k = both(0, s, cols)
        s_all[h % 2, :, s * length : s * length + k.shape[0]] = lax.dot_general(
            q, k, (((1,), (1,)), ((), ())), preferred_element_type=jnp.float32
        )

    def soften(h, r, at):
        used = [s * length + g for s, g in keyed if not hidden(tokens, half, r, at, s, g)]
        for step in range(r * half + at, r * half + at + tokens, 16):
            lines = slice(step, step + 16)
            parts = [
                s_all[h % 2, lines, g : g + 128] + bias_ref[lines, g : g + 128] for g in used
            ]
            top = jnp.max(functools.reduce(jnp.maximum, parts), axis=1, keepdims=True)
            top_ref[h, lines, :] = jnp.broadcast_to(top, (16, HEAD))
            for g, part in zip(used, parts):
                p_all[h % 2, lines, g : g + 128] = jnp.exp2((part - top) * rate).astype(
                    jnp.bfloat16
                )

    def mix(h, r):
        cols = slice(h * HEAD, (h + 1) * HEAD)
        numer = 0.0
        lines = slice(r * half, (r + 1) * half)
        for s in range(n):
            v = both(1, s, cols)
            numer += jnp.dot(
                p_all[h % 2, lines, s * length : s * length + v.shape[0]],
                jnp.concatenate([v, jnp.ones_like(v)], axis=1),
                preferred_element_type=jnp.float32,
            )
        numer_ref[h, lines, :] = numer[:, :HEAD]
        total_ref[h, lines, :] = numer[:, HEAD:]

    for s in range(n):
        score(0, s)
    for h in range(heads):
        for r in range(n):
            if h + 1 < heads:
                score(h + 1, r)
            for at in range(0, half, tokens):
                soften(h, r, at)
            mix(h, r)


def attend_late_kernel(n, cores, tokens, start, count, bias_ref, numer_ref, total_ref, top_ref, *rest):
    own, other, outs = rest[:n], rest[n], rest[n + 1 : -4]
    s_all, p_all, f_all, o_all = rest[-4:]
    z, c = lax.axis_index("tm"), lax.axis_index("sub")
    half = own[0].shape[1]
    heads = own[0].shape[2] // HEAD
    length = half * cores
    t = (z % (n // cores)) * cores + c
    rate = jnp.float32(RATE)
    first = LAST * length + half
    seen = [
        (r, at)
        for r in range(n)
        for at in range(0, half, tokens)
        if not hidden(tokens, half, r, at, LAST, half)
    ]

    def score(h):
        cols = slice(h * HEAD, (h + 1) * HEAD)
        q = jnp.concatenate([own[r][2, at + start : at + start + count, cols] for r, at in seen])
        s_all[h] = lax.dot_general(
            q, other[0, :, cols], (((1,), (1,)), ((), ())), preferred_element_type=jnp.float32
        )

    for h in range(heads):
        score(h)
    for h in range(heads):
        cols = slice(h * HEAD, (h + 1) * HEAD)
        for i, (r, at) in enumerate(seen):
            for step in range(0, count, 16):
                lines = slice(i * count + step, i * count + step + 16)
                base = r * half + at + start + step
                place = slice(base, base + 16)
                parts = [
                    s_all[h, lines, g : g + 128] + bias_ref[place, first + g : first + g + 128]
                    for g in range(0, half, 128)
                ]
                old = top_ref[h, place, :]
                top = jnp.max(functools.reduce(jnp.maximum, parts), axis=1, keepdims=True)
                top = jnp.maximum(old, top)
                f_all[h, lines, :] = jnp.exp2((old - top) * rate)
                for g, part in zip(range(0, half, 128), parts):
                    p_all[h, lines, g : g + 128] = jnp.exp2((part - top[:, :1]) * rate).astype(
                        jnp.bfloat16
                    )
        v = other[1, :, cols]
        added = jnp.dot(
            p_all[h], jnp.concatenate([v, jnp.ones_like(v)], axis=1),
            preferred_element_type=jnp.float32,
        )
        for r in range(n):
            for b, at in enumerate(range(0, half, tokens)):
                place = slice(r * half + at + start, r * half + at + start + count)
                numer, total = numer_ref[h, place, :], total_ref[h, place, :]
                if (r, at) in seen:
                    i = seen.index((r, at)) * count
                    shrink = f_all[h, i : i + count, :]
                    numer = numer * shrink + added[i : i + count, :HEAD]
                    total = total * shrink + added[i : i + count, HEAD:]
                o_all[r, b * count : (b + 1) * count, cols] = (numer / total).astype(jnp.bfloat16)

    for i, out in enumerate(outs):
        out[...] = o_all[t ^ z ^ (n - 1 - i)]


def project_kernel(n, cores, places, own_w, other_w, *rest):
    parts = rest[:n]
    keep_ref, send_ref, a_all = rest[n:]
    z, c, x = lax.axis_index("tm"), lax.axis_index("sub"), lax.axis_index("head")
    count = keep_ref.shape[0]
    for (k, first), part in zip(places, parts):
        for b in range(2):
            at = pl.ds(pl.multiple_of((b ^ 1 ^ x ^ c) * count + first, count), count)
            a_all[z ^ k, b * count : (b + 1) * count] = part[at, :]
    per = n // cores
    wide = a_all.shape[2]
    total = 0.0
    for w_ref, core in ((own_w, c), (other_w, 1 - c)):
        for g in range(per):
            total += jnp.dot(
                a_all[core * per + g], w_ref[g * wide : (g + 1) * wide, :],
                preferred_element_type=jnp.float32,
            )
    send_ref[...] = total[:count].astype(send_ref.dtype)
    keep_ref[...] = total[count:]


def add_kernel(first, keep_ref, got_ref, *rest):
    out_ref, sum_ref, sem = rest[-3:]
    count = keep_ref.shape[0]
    sum_ref[...] = (keep_ref[...] + got_ref[...].astype(jnp.float32)).astype(sum_ref.dtype)
    run_copies([(sum_ref, out_ref.at[0, pl.ds(first, count)])], sem)


def swapped(x, axis):
    return lax.ppermute(x, axis, [(0, 1), (1, 0)])


def spread(n, cores, queries, keys, values, band_table, windows, out_weight):
    _, length, width = queries.shape
    depth, model = out_weight.shape
    wide = width * cores // n
    half = length // cores
    tokens = half // 2
    count = tokens // CHUNKS
    rows = 2 * count
    bf16 = queries.dtype

    def pack(rounds, mb, queries, keys, values):
        return pl.pallas_call(
            functools.partial(pack_kernel, n, cores, tokens, rounds),
            out_shape=[jax.ShapeDtypeStruct((3, half, wide), bf16)] * len(rounds),
            in_specs=[ANY] * 3,
            out_specs=[VMEM] * len(rounds),
            scratch_shapes=[pltpu.SemaphoreType.DMA((4 * len(rounds),))],
            compiler_params=pltpu.CompilerParams(vmem_limit_bytes=mb * 2**20),
            name="pack",
        )(queries, keys, values)

    packed = dict(zip(FIRST, pack(FIRST, PACK_MB, queries, keys, values)))
    others = [r for r in range(n) if r not in FIRST]
    arrays = lax.optimization_barrier((queries, keys, values, packed[FIRST[0]]))[:3]
    packed.update(zip(others, pack(others, PACK_MB, *arrays)))
    per = n // cores
    rounds = [
        [
            (z * cores + c, (c * per + (z ^ r) // cores) * cores + (z ^ r) % cores)
            for z in range(n)
            for c in range(cores)
        ]
        for r in range(n)
    ]
    bias = pl.pallas_call(
        functools.partial(bias_kernel, n, cores, tokens),
        out_shape=jax.ShapeDtypeStruct((n * half, n * length), jnp.float32),
        in_specs=[SMEM, SMEM],
        out_specs=VMEM,
        compiler_params=pltpu.CompilerParams(vmem_limit_bytes=4 * 2**20),
        name="bias",
    )(band_table, windows)
    blocks = [packed[r] for r in range(n)]
    blocks[TIE], _ = lax.optimization_barrier((packed[TIE], bias))
    own = [lax.ppermute(blocks[r], ("tm", "sub"), rounds[r]) for r in range(n)]
    weight, _ = lax.optimization_barrier((out_weight, packed[W_AFTER]))
    other_weight = swapped(weight, "sub")
    other = []
    for r in range(n):
        other.append(swapped(own[r], "sub"))
    bias, other_weight = lax.optimization_barrier((bias, other_weight))

    heads = wide // HEAD
    f32 = jnp.float32
    partial = pl.pallas_call(
        functools.partial(attend_early_kernel, n, cores, tokens),
        out_shape=[jax.ShapeDtypeStruct((heads, n * half, HEAD), f32)] * 3,
        in_specs=[VMEM] * (2 * n),
        out_specs=[VMEM] * 3,
        scratch_shapes=[
            pltpu.VMEM((2, n * half, n * length), f32),
            pltpu.VMEM((2, n * half, n * length), bf16),
        ],
        compiler_params=pltpu.CompilerParams(vmem_limit_bytes=24 * 2**20),
        name="attend_early",
    )(bias, *own, *other[1:])
    blocks_seen = 2 * n if tokens < ACROSS else n + 1
    back = []
    for a in range(CHUNKS):
        outs = pl.pallas_call(
            functools.partial(attend_late_kernel, n, cores, tokens, a * count, count),
            out_shape=[jax.ShapeDtypeStruct((rows, wide), bf16)] * n,
            in_specs=[VMEM] * (5 + n),
            out_specs=[VMEM] * n,
            scratch_shapes=[
                pltpu.VMEM((heads, blocks_seen * count, half), f32),
                pltpu.VMEM((heads, blocks_seen * count, half), bf16),
                pltpu.VMEM((heads, blocks_seen * count, HEAD), f32),
                pltpu.VMEM((n, rows, wide), bf16),
            ],
            compiler_params=pltpu.CompilerParams(vmem_limit_bytes=24 * 2**20),
            name="attend_late",
        )(bias, *partial, *own, other[0])
        for i, out in enumerate(outs):
            k = n - 1 - i
            pairs = [(z, z ^ k) for z in range(n)]
            back.append((k, [a], lax.ppermute(out, "tm", pairs) if k else out))
    sums = []
    for a in range(CHUNKS):
        held = [(k, chunks.index(a) * rows, part) for k, chunks, part in back if a in chunks]
        places = [(k, first) for k, first, _ in held]
        parts = [part for _, _, part in held]
        keep, send = pl.pallas_call(
            functools.partial(project_kernel, n, cores, places),
            out_shape=[
                jax.ShapeDtypeStruct((count, model), jnp.float32),
                jax.ShapeDtypeStruct((count, model), bf16),
            ],
            in_specs=[VMEM] * (2 + n),
            out_specs=[VMEM] * 2,
            scratch_shapes=[pltpu.VMEM((n, rows, wide), bf16)],
            compiler_params=pltpu.CompilerParams(vmem_limit_bytes=24 * 2**20),
            name="project",
        )(out_weight, other_weight, *parts)
        sums += [keep, swapped(send, "head")]
    mixed = []
    for a in range(CHUNKS):
        mixed = [
            pl.pallas_call(
                functools.partial(add_kernel, a * count),
                out_shape=jax.ShapeDtypeStruct((1, tokens, model), bf16),
                in_specs=[VMEM] * 2 + [ANY] * len(mixed),
                out_specs=ANY,
                scratch_shapes=[
                    pltpu.VMEM((count, model), bf16),
                    pltpu.SemaphoreType.DMA((1,)),
                ],
                input_output_aliases={2: 0} if mixed else {},
                compiler_params=pltpu.CompilerParams(vmem_limit_bytes=4 * 2**20),
                name="add",
            )(*sums[2 * a : 2 * a + 2], *mixed)
        ]
    return mixed[0]


def solution(mesh):
    n, cores, xs = mesh.shape["tm"], mesh.shape["sub"], mesh.shape["head"]

    def local(queries, keys, values, band_table, windows, out_weight):
        frames, length, width = queries.shape
        fits = (
            frames == 1
            and n > 2
            and n & (n - 1) == 0
            and cores == 2
            and xs == 2
            and n % cores == 0
            and width * cores % (n * HEAD) == 0
            and length % (xs * cores * CHUNKS * 16) == 0
        )
        step = functools.partial(spread, n, cores) if fits else gathered
        return step(queries, keys, values, band_table, windows, out_weight)

    return jax.shard_map(
        local,
        mesh=mesh,
        in_specs=(
            P(("clip", "tm"), None, ("head", "sub")),
            P(("clip", "tm"), None, ("head", "sub")),
            P(("clip", "tm"), None, ("head", "sub")),
            P(),
            P(),
            P(("head", "sub"), None),
        ),
        out_specs=P(("clip", "tm"), ("head", "sub"), None),
        check_vma=False,
    )
```
